32 devices in a mesh: section: 2 (over core), expert: 16 (over z, y, x).
Axes of the slice: x: 2, y: 2, z: 4, core: 2. Of those that a mesh axis runs over, the one named last changes fastest.
Arguments:
- block_input: bfloat16 [2, 6144, 768], P(None, 'expert'), may hold values from -6 to 6
- cotangent: bfloat16 [2, 6144, 768], P(None, 'expert'), may hold values from -6 to 6
- lengths: int32 [2, 16, 4], P(None, 'expert'), may hold values from 1 to 288, 384 in all within a row
- routes: int32 [2, 2, 6144, 1], P('section', None, 'expert'), may hold values from 0 to 15; in each aligned block of 384 rows (0 to 383, 384 to 767, ..., all dimensions but the last counted through in order) at most 36 rows name the same one
- norm_gain: float32 [2, 2, 768], P('section'), may hold values from 0.5 to 1.5
- attention_in: bfloat16 [2, 3, 768, 768], P('section', None, 'expert'), may hold values from -0.21875 to 0.21875
- attention_out: bfloat16 [2, 768, 768], P('section', 'expert'), may hold values from -0.875 to 0.875
- position_bias: float32 [2, 32, 12], P('section'), may hold values from -6 to 6
- router: bfloat16 [2, 768, 16], P('section', 'expert'), may hold values from -0.109375 to 0.109375
- expert_up: bfloat16 [2, 16, 768, 3072], P('section', 'expert'), may hold values from -0.21875 to 0.21875
- expert_down: bfloat16 [2, 16, 3072, 768], P('section', 'expert'), may hold values from -3.5 to 3.5
Outputs:
- layer_out: bfloat16 [2, 2, 6144, 768], P('section', None, 'expert')
- input_grad: float32 [2, 2, 6144, 768], P('section', None, 'expert')
- grad_gain: float32 [2, 2, 768], P('section')
- grad_attention_in: float32 [2, 3, 768, 768], P('section', None, 'expert')
- grad_attention_out: float32 [2, 768, 768], P('section', 'expert')
- grad_position_bias: float32 [2, 32, 12], P('section')
- grad_router: float32 [2, 768, 16], P('section', 'expert')
- grad_expert_up: float32 [2, 16, 768, 3072], P('section', 'expert')
- grad_expert_down: float32 [2, 16, 3072, 768], P('section', 'expert')
The draws below stay inside these ranges and needn't reach their ends.
Inputs may be any that keep to these rules, and one draw needn't show every extreme that they name: Each row holds the lengths of the 4 sequences of one group of one micro-batch; they sum to 384, and the longest in each row is exactly 288. routes[s, m, t, 0] is the expert that token t of micro-batch m uses in section s. Among the 384 tokens of one group of one micro-batch (the rows of one device, aligned blocks), no expert is named more than 36 times, and in every draw some group names one expert exactly 36 times.
All inputs are finite; a program needn't handle non-finite values.
Results may differ from the reference program's by a relative error of at most 0.023.
Values may be sent and summed in bfloat16 or wider, within the bound.
No kernel may reach another device: no remote copies, remote signals or barrier semaphores. Data moves between devices by JAX's collectives and lax.ppermute only.
A program may use at most 320 MiB of HBM per device.

```python
import math
import jax
import jax.numpy as jnp
import numpy as np
from jax import lax

D = 768
HEADS = 12
FF = 3072
BUCKETS = 32
TOK_MB = 384
MICRO = 2
SEQS = 4
SECTIONS = 2
GROUPS = 16
EXPERTS = 16
TOKENS = 6144
CAP = 36
N_EXPERT = 16


def level_of(own_key, extent, shards, smallest, high):
    factor_of = 1.0
    for dim, blocks in shards:
        steps = jax.random.uniform(jax.random.fold_in(jax.random.fold_in(own_key, 6), dim), (blocks,), jnp.float32, smallest / len(shards), high / len(shards))
        factor_of = factor_of * jnp.repeat(jnp.exp(steps), extent[dim] // blocks).reshape((-1,) + (1,) * (len(extent) - 1 - dim))
    return factor_of


def split_up(amount, total, bound, slope):
    weights = [(1 << 20) // math.isqrt(rank ** slope) + 1 for rank in range(2, amount + 1)]
    surplus, counts = total - bound - (amount - 1), [1] * (amount - 1)
    while surplus > 0:
        candidates = [i for i in range(amount - 1) if counts[i] < bound]
        whole, left = sum([weights[i] for i in candidates]), surplus
        for i in candidates:
            extra = min(bound - counts[i], max(1, left * weights[i] // whole), surplus)
            counts[i] = counts[i] + extra
            surplus = surplus - extra
    return np.array([bound] + counts)


def uneven(rng, count, total, most, slope):
    if count == 2:
        one = jax.random.randint(rng, (), max(1, total - most), min(most, total - 1) + 1)
        return jnp.stack([one, total - one])
    tallies = jnp.asarray(split_up(count, total, most, slope), jnp.int32)
    couples = (count - 1) // 2
    source_of, taker = tallies[1:1 + 2 * couples:2], tallies[2:2 + 2 * couples:2]
    room = jnp.minimum(source_of - 1, most - taker)
    shifted = jax.random.randint(jax.random.fold_in(rng, 1), (couples,), 0, 1 << 20) % (room + 1)
    tallies = tallies.at[1:1 + 2 * couples:2].set(source_of - shifted).at[2:2 + 2 * couples:2].set(taker + shifted)
    return tallies[jax.random.permutation(jax.random.fold_in(rng, 2), count)]


def shared_out(rng, own, number, rows, count, top, reach, slope):
    order = jax.random.permutation(rng, count)
    packed, common = portions_of(count, rows * top, reach, slope, True), portions_of(count, rows * top, reach, slope, False)
    places = jnp.arange(count)

    def named(sizes, rotation):
        used = int((sizes > 0).sum())
        fixed = max(1, used // 4)
        moved = fixed + (places - fixed + rotation * (used - fixed)) % max(1, count - fixed)
        return jnp.zeros((count,), jnp.int32).at[order[jnp.where(places < fixed, places, moved)]].set(jnp.asarray(sizes, jnp.int32))

    sizes = jnp.where(number % 4 == 0, named(packed, number // 4), named(common, number - number // 4 - 1))
    mixed = jax.random.permutation(jax.random.fold_in(own, 3), count)
    giver, sink = mixed[0:count // 2 * 2:2], mixed[1:count // 2 * 2:2]
    slack = jnp.minimum(sizes[giver] - 1, reach - sizes[sink]) // 2
    slack = jnp.where((giver == order[0]) | (sink == order[0]) | (sizes[sink] == 0), 0, jnp.maximum(slack, 0))
    moved = jax.random.randint(jax.random.fold_in(own, 4), (count // 2,), 0, 1 << 20) % (slack + 1)
    sizes = sizes.at[giver].add(-moved).at[sink].add(moved)
    labels = jnp.searchsorted(jnp.cumsum(sizes), jnp.arange(rows * top), side="right").astype(jnp.int32)
    grid = labels.reshape(top, rows).T
    grid = grid[jax.random.permutation(jax.random.fold_in(own, 1), rows)]
    rotation = jax.random.randint(jax.random.fold_in(own, 2), (rows, 1), 0, top)
    return jnp.take_along_axis(grid, (jnp.arange(top)[None, :] + rotation) % top, axis=1)


def portions_of(amount, total, limit, skew, full):
    portions = [(1 << 20) // math.isqrt(standing ** skew) + 1 for standing in range(1, amount + 1)]
    largest = limit if full else min(limit, max(-(-total // amount), total * portions[0] // sum(portions)))
    least = 1 if total - largest >= amount - 1 else 0
    counts, rest = [largest] + [least] * (amount - 1), total - largest - least * (amount - 1)
    while rest > 0:
        free = [i for i in range(1, amount) if counts[i] < largest] or [i for i in range(1, amount) if counts[i] < limit]
        whole, budget = sum([portions[i] for i in free]), rest
        for i in free:
            addition = min(limit - counts[i], max(1, budget * portions[i] // whole), rest)
            counts[i] = counts[i] + addition
            rest = rest - addition
    return np.array(counts)


def normal_values(own_key, dims, deviation, reach, cuts=(), kind=jnp.bfloat16):
    result = deviation * jax.random.normal(own_key, dims, jnp.float32)
    if cuts:
        result = result * level_of(own_key, dims, cuts, -0.22, 0.18)
    return jnp.clip(result, -reach, reach).astype(kind)


def setup_inputs(seed: int = 0) -> dict:
    key_list = jax.random.split(jax.random.key(seed), 12)
    block_input = normal_values(key_list[0], (MICRO, TOKENS, D), 1.0, 6.0, ((1, 16),))
    cotangent = normal_values(key_list[1], (MICRO, TOKENS, D), 1.0, 6.0, ((1, 16),))
    lengths = jax.vmap(lambda own: uneven(own, SEQS, TOK_MB, TOK_MB * 3 // 4, 2))(jax.random.split(key_list[2], MICRO * GROUPS)).reshape((MICRO, GROUPS, SEQS)).astype(jnp.int32)
    routes_keys = jax.random.split(jax.random.fold_in(key_list[3], 1), SECTIONS * MICRO * TOKENS // TOK_MB)
    routes_turns = jax.random.permutation(jax.random.fold_in(key_list[3], 3), SECTIONS * MICRO * TOKENS // TOK_MB)
    routes = jax.vmap(lambda own, number: shared_out(jax.random.fold_in(key_list[3], 2), own, number, TOK_MB, EXPERTS, 1, CAP, 2))(routes_keys, routes_turns).reshape((SECTIONS, MICRO, TOKENS, 1))
    norm_gain = jnp.clip(1.0 + 0.1 * jax.random.normal(key_list[4], (SECTIONS, 2, D), jnp.float32), 0.5, 1.5)
    attention_in = normal_values(key_list[5], (SECTIONS, 3, D, D), D ** -0.5, 0.21875, ((0, 2), (2, 16)))
    attention_out = normal_values(key_list[6], (SECTIONS, D, D), (D // 16) ** -0.5, 0.875, ((0, 2), (1, 16)))
    position_bias = normal_values(key_list[7], (SECTIONS, BUCKETS, HEADS), 1.0, 6.0, ((0, 2),), jnp.float32)
    router = normal_values(key_list[8], (SECTIONS, D, EXPERTS), (4 * D) ** -0.5, 0.109375, ((0, 2), (1, 16)))
    expert_up = normal_values(key_list[9], (SECTIONS, EXPERTS, D, FF), D ** -0.5, 0.21875, ((0, 2), (1, 16)))
    expert_down = normal_values(key_list[10], (SECTIONS, EXPERTS, FF, D), (EXPERTS * 2 * FF ** -0.5), 3.5, ((0, 2), (1, 16)))
    return dict(block_input=block_input, cotangent=cotangent, lengths=lengths, routes=routes, norm_gain=norm_gain, attention_in=attention_in, attention_out=attention_out, position_bias=position_bias, router=router, expert_up=expert_up, expert_down=expert_down)


bucket_edges = (12, 16, 23, 32, 46, 64, 91)
norm_eps = 1e-06
gelu_c = 0.7978845608028654
gelu_cube = 0.044715
masked_score = -1e+30
highest = lax.Precision.HIGHEST

@jax.custom_vjp
def low(v):
    return lax.optimization_barrier(v.astype(jnp.bfloat16)).astype(jnp.float32)

@jax.custom_vjp
def low_back(v):
    return v

def low_keep(v):
    return (low(v), None)

def low_pass(kept, grad):
    return (grad,)

def back_keep(v):
    return (v, None)

def back_low(kept, grad):
    return (low(grad),)
low.defvjp(low_keep, low_pass)
low_back.defvjp(back_keep, back_low)

def gelu(value):
    return 0.5 * value * (1.0 + jnp.tanh(gelu_c * (value + gelu_cube * value * value * value)))

def bucket_of(offset):
    distance = jnp.abs(offset)
    found = 16 * (offset > 0).astype(jnp.int32) + jnp.minimum(distance, 8)
    for edge in bucket_edges:
        found = found + (distance >= edge).astype(jnp.int32)
    return found

def normed(values, gain):
    return values * lax.rsqrt(lax.optimization_barrier(jnp.mean(values * values, axis=-1, keepdims=True)) + norm_eps) * gain

def softmax_rows(scores):
    top = lax.optimization_barrier(jnp.max(scores, axis=-1, keepdims=True))
    raised = jnp.exp(scores - top)
    return raised / lax.optimization_barrier(jnp.sum(raised, axis=-1, keepdims=True))

def attend(normed_low, segment, project_in, project_out, table, buckets):
    rows = normed_low.shape[0]
    heads = table.shape[1]

    def split(weight):
        return low_back(low(jnp.dot(normed_low, weight, precision=highest))).reshape(rows, heads, -1)
    queries = split(project_in[0])
    keys = split(project_in[1])
    values = split(project_in[2])
    bias = jnp.transpose(jnp.take(table, buckets, axis=0), (2, 0, 1))
    scale = queries.shape[-1] ** (-0.5)
    scores = jnp.einsum('ihd,jhd->hij', queries, keys, precision=highest) * scale + bias
    scores = low_back(scores)
    same = segment[:, None] == segment[None, :]
    scores = jnp.where(same[None], scores, masked_score)
    shares = low(softmax_rows(scores))
    mixed = jnp.einsum('hij,jhd->ihd', shares, values, precision=highest).reshape(rows, -1)
    mixed = low_back(low(mixed))
    return low_back(jnp.dot(mixed, project_out, precision=highest))

def layer(inputs, weights, section, route, segment, buckets):
    gains = weights[0][section]
    project_in = weights[1][section]
    project_out = weights[2][section]
    table = weights[3][section]
    router_weight = weights[4][section]
    up_weight = weights[5][section]
    down_weight = weights[6][section]
    blocks = inputs.shape[0] // TOK_MB
    normed_one = low(normed(inputs, gains[0]))

    def block_attention(pair):
        return attend(pair[0], pair[1], project_in, project_out, table, buckets)
    attended = lax.map(jax.checkpoint(block_attention), (normed_one.reshape(blocks, TOK_MB, D), segment.reshape(blocks, TOK_MB)))
    middle = inputs + attended.reshape(inputs.shape)
    normed_two = low(normed(middle, gains[1]))
    logits = low_back(jnp.dot(normed_two, router_weight, precision=highest))
    shares = softmax_rows(logits)
    chosen = route[:, None] == jnp.arange(EXPERTS, dtype=jnp.int32)[None, :]
    gate = lax.optimization_barrier(jnp.sum(jnp.where(chosen, shares, 0.0), axis=1, keepdims=True))
    chosen_int = chosen.astype(jnp.int32).reshape(blocks, TOK_MB, EXPERTS)
    earlier = (jnp.cumsum(chosen_int, axis=1) - chosen_int).reshape(-1, EXPERTS)
    slot = lax.optimization_barrier(jnp.sum(jnp.where(chosen, earlier, 0), axis=1))
    column = jnp.arange(inputs.shape[0], dtype=jnp.int32) // TOK_MB * CAP + slot
    buffer = jnp.zeros((EXPERTS, N_EXPERT * CAP, D), jnp.float32).at[route, column].set(normed_two)
    buffer = low_back(buffer)
    pre_gelu = low_back(jnp.einsum('erd,edf->erf', buffer, up_weight, precision=highest))
    active = low(gelu(pre_gelu))
    returned = low_back(low(jnp.einsum('erf,efd->erd', active, down_weight, precision=highest)))
    combined = returned[route, column]
    return middle + gate * combined

def reference(block_input, cotangent, lengths, routes, norm_gain, attention_in, attention_out, position_bias, router, expert_up, expert_down):
    positions = jnp.arange(TOK_MB, dtype=jnp.int32)
    buckets = bucket_of(positions[None, :] - positions[:, None])
    bounds = jnp.cumsum(lengths, axis=-1)
    segment = lax.optimization_barrier(jnp.sum((positions[None, None, :, None] >= bounds[:, :, None, :]).astype(jnp.int32), axis=-1)).reshape(MICRO, TOKENS)
    weights = (norm_gain.astype(jnp.float32), attention_in.astype(jnp.float32), attention_out.astype(jnp.float32), position_bias.astype(jnp.float32), router.astype(jnp.float32), expert_up.astype(jnp.float32), expert_down.astype(jnp.float32))
    inputs = block_input.astype(jnp.float32)
    bridge = jnp.zeros((MICRO, TOKENS, D), jnp.float32)

    def forward(weights, inputs, bridge):
        firsts = []
        seconds = []
        for which in range(MICRO):
            one = layer(inputs[which], weights, 0, routes[0, which, :, 0], segment[which], buckets)
            passed = low_back(low(one)) + bridge[which]
            two = layer(passed, weights, 1, routes[1, which, :, 0], segment[which], buckets)
            firsts.append(one)
            seconds.append(two)
        return (jnp.stack(firsts), jnp.stack(seconds))
    (firsts, seconds), pullback = jax.vjp(forward, weights, inputs, bridge)
    grads, grad_inputs, grad_bridge = pullback((jnp.zeros_like(firsts), cotangent.astype(jnp.float32)))
    layer_out = jnp.stack([firsts, seconds]).astype(jnp.bfloat16)
    input_grad = jnp.stack([grad_inputs, grad_bridge])
    return (layer_out, input_grad, grads[0], grads[1], grads[2], grads[3], grads[4], grads[5], grads[6])
```

```python
import functools

import jax
import jax.numpy as jnp
from jax import lax
from jax.experimental import pallas as pl
from jax.experimental.pallas import tpu as pltpu
from jax.sharding import PartitionSpec as P

bucket_edges = (12, 16, 23, 32, 46, 64, 91)
norm_eps = 1e-06
gelu_c = 0.7978845608028654
gelu_cube = 0.044715
masked_score = -1e30
highest = lax.Precision.HIGHEST
f32 = jnp.float32
bf16 = jnp.bfloat16
vmem_bytes = 56 * 2**20
pieces = 3


def dot(left, right):
    return jnp.dot(left, right, preferred_element_type=f32)


def dot_lead(left, right):
    return lax.dot_general(left, right, (((0,), (0,)), ((), ())), preferred_element_type=f32)


def dot_last(left, right):
    return lax.dot_general(left, right, (((1,), (1,)), ((), ())), preferred_element_type=f32)


def gelu_pair(value):
    square = value * value
    inner = jnp.tanh(gelu_c * value * (1.0 + gelu_cube * square))
    half = 0.5 * (1.0 + inner)
    slope = half + 0.5 * value * (1.0 - inner * inner) * (
        gelu_c * (1.0 + 3.0 * gelu_cube * square)
    )
    return (value * half, slope)


def bucket_of(offset):
    distance = jnp.abs(offset)
    found = 16 * (offset > 0).astype(jnp.int32) + jnp.minimum(distance, 8)
    for edge in bucket_edges:
        found = found + (distance >= edge).astype(jnp.int32)
    return found


def norm_scale(values):
    return lax.rsqrt(jnp.mean(values * values, axis=-1, keepdims=True) + norm_eps)


def norm_backward(values, gain, grad_normed):
    scale = norm_scale(values)
    normal = values * scale
    inner = grad_normed * gain
    grad_values = scale * (inner - normal * jnp.mean(inner * normal, axis=-1, keepdims=True))
    return (grad_values, jnp.sum(grad_normed * normal, axis=0, keepdims=True))


def weight_copies(core, own, other, weights, sems):
    copies = []
    step = weights.shape[2] // len(own)
    for p in range(len(own)):
        columns = pl.ds(p * step, step)
        for which, (ref, at) in enumerate(((own[p], 2 * core), (other[p], 2 - 2 * core))):
            copies.append(
                pltpu.make_async_copy(
                    ref, weights.at[pl.ds(at, 2), :, columns], sems.at[2 * p + which]
                )
            )
    for copy in copies:
        copy.start()
    return copies


def head_masks():
    lane = lax.broadcasted_iota(jnp.int32, (1, 128), 1)
    low = (lane < 64).astype(f32)
    return (low, 1.0 - low)


def bias_of(line_ref, head, rows):
    line = jnp.broadcast_to(line_ref[pl.ds(head, 1), :], (rows, 2 * rows))
    return pltpu.roll(line, rows + 1, 1, stride=1, stride_axis=0)[:, :rows]


def one_hot_columns(place_col, slots):
    rows = place_col.shape[0]
    return (place_col == lax.broadcasted_iota(jnp.int32, (rows, slots), 1)).astype(f32).astype(bf16)


def one_hot_rows(place_row, slots):
    rows = place_row.shape[1]
    return (place_row == lax.broadcasted_iota(jnp.int32, (slots, rows), 0)).astype(f32).astype(bf16)


def forward_kernel(second, core_ref, *refs):
    own, refs = refs[:pieces], refs[pieces:]
    other, refs = refs[:pieces], refs[pieces:]
    if second:
        (before_ref, gate_before_ref, place_before_ref, back_ref, cot_ref), refs = refs[:5], refs[5:]
    else:
        (x_ref,), refs = refs[:1], refs[1:]
    (gain_ref, router_ref, line_ref, seg_col_ref, seg_row_ref, route_ref, place_ref), refs = (
        refs[:7],
        refs[7:],
    )
    (q_ref, k_ref, v_ref, o_ref, lse_ref, mid_ref, h2_ref, share_ref, gate_ref, send_ref), refs = (
        refs[:10],
        refs[10:],
    )
    if second:
        (x_out_ref, combined_ref, grad_send_ref), refs = refs[:3], refs[3:]
    weights, sems = refs
    copies = weight_copies(core_ref[0], own, other, weights, sems)
    slots = send_ref.shape[0]
    rows = q_ref.shape[0]
    if second:
        scatter = one_hot_columns(place_before_ref[...], slots)
        combined = dot(scatter, back_ref[...])
        combined_ref[...] = combined.astype(bf16)
        low = (before_ref[...] + gate_before_ref[...] * combined).astype(bf16)
        x_out_ref[...] = low
        wide = low.astype(f32)
    else:
        wide = x_ref[...].astype(f32)
    h1 = (wide * norm_scale(wide) * gain_ref[0:1, :]).astype(bf16)
    for copy in copies:
        copy.wait()
    q_ref[...] = dot(h1, weights[0]).astype(bf16)
    k_ref[...] = dot(h1, weights[1]).astype(bf16)
    v_ref[...] = dot(h1, weights[2]).astype(bf16)
    same = seg_col_ref[...] == seg_row_ref[...]
    masks = head_masks()
    lanes = lax.broadcasted_iota(jnp.int32, (rows, 128), 1)

    def pair(p, lse):
        columns = pl.ds(pl.multiple_of(p * 128, 128), 128)
        queries, keys, values = q_ref[:, columns], k_ref[:, columns], v_ref[:, columns]
        mixed = jnp.zeros((rows, 128), f32)
        for half in range(2):
            head = 2 * p + half
            low_mask = masks[half].astype(bf16)
            scores = dot_last(queries * low_mask, keys) * 0.125 + bias_of(line_ref, head, rows)
            scores = jnp.where(same, scores, masked_score)
            top = jnp.max(scores, axis=-1, keepdims=True)
            raised = jnp.exp(scores - top)
            total = jnp.sum(raised, axis=-1, keepdims=True)
            shares = (raised * (1.0 / total)).astype(bf16)
            mixed = mixed + dot(shares, values * low_mask)
            lse = jnp.where(lanes == head, top + jnp.log(total), lse)
        o_ref[:, columns] = mixed.astype(bf16)
        return lse

    lse_ref[...] = lax.fori_loop(0, line_ref.shape[0] // 2, pair, jnp.zeros((rows, 128), f32))
    middle = wide + dot(o_ref[...], weights[3])
    mid_ref[...] = middle
    h2 = (middle * norm_scale(middle) * gain_ref[1:2, :]).astype(bf16)
    h2_ref[...] = h2
    logits = dot(h2, router_ref[...])
    raised = jnp.exp(logits - jnp.max(logits, axis=-1, keepdims=True))
    shares = raised / jnp.sum(raised, axis=-1, keepdims=True)
    share_ref[...] = shares
    chosen = route_ref[...] == lax.broadcasted_iota(jnp.int32, shares.shape, 1)
    gate = jnp.sum(jnp.where(chosen, shares, 0.0), axis=-1, keepdims=True)
    gate_ref[...] = gate
    gather = one_hot_rows(place_ref[...], slots)
    send_ref[...] = dot(gather, h2).astype(bf16)
    if second:
        grad_out = (gate * cot_ref[...].astype(f32)).astype(bf16)
        grad_send_ref[...] = dot(gather, grad_out).astype(bf16)


def backward_kernel(second, core_ref, *refs):
    own, refs = refs[:pieces], refs[pieces:]
    other, refs = refs[:pieces], refs[pieces:]
    (
        x_ref, q_ref, k_ref, v_ref, o_ref, lse_ref, mid_ref, h2_ref, share_ref, gate_ref,
        dy_ref, dback_ref, out_ref, gain_ref, router_ref, line_ref, seg_col_ref, seg_row_ref,
        route_ref, place_ref,
    ), refs = refs[:20], refs[20:]
    if second:
        (gate_next_ref, place_next_ref), refs = refs[:2], refs[2:]
    (dx_ref, keep_ref, give_ref, router_grad_ref, gain_grad_ref, line_grad_ref), refs = (
        refs[:6],
        refs[6:],
    )
    if second:
        (y_ref, grad_send_ref), refs = refs[:2], refs[2:]
    weights, do_ref, dq_ref, dk_ref, dv_ref, dx1_ref, sems = refs
    core = core_ref[0]
    copies = weight_copies(core, own, other, weights, sems)
    rows = q_ref.shape[0]
    slots = dback_ref.shape[0]

    def put(matrix, value):
        value = value.astype(bf16)

        @pl.when(core == matrix // 2)
        def _():
            keep_ref[matrix % 2] = value

        @pl.when(core != matrix // 2)
        def _():
            give_ref[matrix % 2] = value

    dy = dy_ref[...].astype(f32)
    gate = gate_ref[...]
    middle = mid_ref[...]
    scatter = one_hot_columns(place_ref[...], slots)
    if second:
        combined = dot(scatter, out_ref[...])
        y_ref[...] = (middle + gate * combined).astype(bf16)
    else:
        combined = out_ref[...].astype(f32)
    grad_gate = jnp.sum(dy * combined, axis=-1, keepdims=True)
    shares = share_ref[...]
    chosen = route_ref[...] == lax.broadcasted_iota(jnp.int32, shares.shape, 1)
    grad_logits = (grad_gate * gate * (chosen.astype(f32) - shares)).astype(bf16)
    router_grad_ref[...] = dot_lead(h2_ref[...], grad_logits)
    grad_two = dot(scatter, dback_ref[...]) + dot_last(grad_logits, router_ref[...])
    grad_middle, gain_two = norm_backward(middle, gain_ref[1:2, :], grad_two)
    grad_middle = grad_middle + dy
    dx1_ref[...] = grad_middle
    low = grad_middle.astype(bf16)
    for copy in copies:
        copy.wait()
    put(3, dot_lead(o_ref[...], low))
    do_ref[...] = dot_last(low, weights[3]).astype(bf16)
    same = seg_col_ref[...] == seg_row_ref[...]
    masks = head_masks()
    lanes = lax.broadcasted_iota(jnp.int32, (rows, 128), 1)
    flip = (
        lax.broadcasted_iota(jnp.int32, (rows, rows), 0)
        + lax.broadcasted_iota(jnp.int32, (rows, rows), 1)
        == rows - 1
    )
    flip = flip.astype(f32).astype(bf16)

    def pair(p, carry):
        columns = pl.ds(pl.multiple_of(p * 128, 128), 128)
        queries, keys, values = q_ref[:, columns], k_ref[:, columns], v_ref[:, columns]
        grad_mixed = do_ref[:, columns]
        dq = jnp.zeros((rows, 128), f32)
        dk = jnp.zeros((rows, 128), f32)
        dv = jnp.zeros((rows, 128), f32)
        for half in range(2):
            head = 2 * p + half
            low_mask = masks[half].astype(bf16)
            own_queries = queries * low_mask
            own_mixed = grad_mixed * low_mask
            lse = jnp.sum(jnp.where(lanes == head, lse_ref[...], 0.0), axis=-1, keepdims=True)
            scores = dot_last(own_queries, keys) * 0.125 + bias_of(line_ref, head, rows)
            shares = jnp.exp(jnp.where(same, scores, masked_score) - lse)
            grad_shares = dot_last(own_mixed, values)
            mean = jnp.sum(shares * grad_shares, axis=-1, keepdims=True)
            grad_scores = (shares * (grad_shares - mean)).astype(bf16)
            dv = dv + dot_lead(shares.astype(bf16), own_mixed)
            dq = dq + dot(grad_scores, keys * low_mask)
            dk = dk + dot_lead(grad_scores, own_queries)
            flipped = dot(flip, grad_scores)
            wide = jnp.concatenate([flipped, jnp.zeros_like(flipped)], axis=1)
            turned = pltpu.roll(wide, 0, 1, stride=1, stride_axis=0)
            line_grad_ref[pl.ds(head, 1), :] = jnp.sum(turned, axis=0, keepdims=True)
        dq_ref[:, columns] = (dq * 0.125).astype(bf16)
        dk_ref[:, columns] = (dk * 0.125).astype(bf16)
        dv_ref[:, columns] = dv.astype(bf16)
        return carry

    lax.fori_loop(0, line_ref.shape[0] // 2, pair, 0)
    wide = x_ref[...].astype(f32)
    grad_one = (
        dot_last(dq_ref[...], weights[0])
        + dot_last(dk_ref[...], weights[1])
        + dot_last(dv_ref[...], weights[2])
    )
    grad_inputs, gain_one = norm_backward(wide, gain_ref[0:1, :], grad_one)
    grad_inputs = grad_inputs + dx1_ref[...]
    dx_ref[...] = grad_inputs
    gain_grad_ref[0:1, :] = gain_one
    gain_grad_ref[1:2, :] = gain_two
    if second:
        grad_out = (gate_next_ref[...] * grad_inputs.astype(bf16).astype(f32)).astype(bf16)
        gather = one_hot_rows(place_next_ref[...], slots)
        grad_send_ref[...] = dot(gather, grad_out).astype(bf16)
    h1 = (wide * norm_scale(wide) * gain_ref[0:1, :]).astype(bf16)
    put(0, dot_lead(h1, dq_ref[...]))
    put(1, dot_lead(h1, dk_ref[...]))
    put(2, dot_lead(h1, dv_ref[...]))


def expert_copies(mine, tiles, up_refs, down_refs, up, down, sems, start):
    width = up.shape[2]

    def copies(which):
        found = []
        for j in range(tiles):
            at = pl.ds(j * width, width)
            found.append(
                (
                    pltpu.make_async_copy(up_refs[which].at[:, at], up.at[j], sems.at[0, j]),
                    pltpu.make_async_copy(down_refs[which].at[at, :], down.at[j], sems.at[1, j]),
                )
            )
        return found

    if start:
        for which in range(2):

            @pl.when(mine == 1 - which)
            def _():
                for couple in copies(which):
                    for copy in couple:
                        copy.start()


def expert_wait(j, up_ref, down_ref, up, down, sems):
    width = up.shape[2]
    at = pl.ds(0, width)
    pltpu.make_async_copy(up_ref.at[:, at], up.at[j], sems.at[0, j]).wait()
    pltpu.make_async_copy(down_ref.at[at, :], down.at[j], sems.at[1, j]).wait()


def expert_forward_kernel(
    mine_ref, x_ref, up_own, up_other, down_own, down_other, act_ref, slope_ref, out_ref,
    up, down, total, sems,
):
    j = pl.program_id(0)
    tiles = up.shape[0]

    @pl.when(j == 0)
    def _():
        expert_copies(
            mine_ref[0], tiles, (up_own, up_other), (down_own, down_other), up, down, sems, True
        )
        total[...] = jnp.zeros_like(total)

    expert_wait(j, up_own, down_own, up, down, sems)
    active, slope = gelu_pair(dot(x_ref[...], up[j]))
    active = active.astype(bf16)
    act_ref[...] = active
    slope_ref[...] = slope.astype(bf16)
    total[...] += dot(active, down[j])

    @pl.when(j == tiles - 1)
    def _():
        out_ref[...] = total[...].astype(bf16)


def expert_backward_kernel(
    mine_ref, dout_ref, slope_ref, up_own, up_other, down_own, down_other, dpre_ref, dbuf_ref,
    up, down, total, sems,
):
    j = pl.program_id(0)
    tiles = up.shape[0]

    @pl.when(j == 0)
    def _():
        expert_copies(
            mine_ref[0], tiles, (up_own, up_other), (down_own, down_other), up, down, sems, True
        )
        total[...] = jnp.zeros_like(total)

    expert_wait(j, up_own, down_own, up, down, sems)
    grad_pre = (dot_last(dout_ref[...], down[j]) * slope_ref[...].astype(f32)).astype(bf16)
    dpre_ref[...] = grad_pre
    total[...] += dot_last(grad_pre, up[j])

    @pl.when(j == tiles - 1)
    def _():
        dbuf_ref[...] = total[...].astype(bf16)


def up_grad_kernel(buf_a, buf_b, dpre_a, dpre_b, grad_ref):
    grad_ref[...] = dot_lead(buf_a[...], dpre_a[...]) + dot_lead(buf_b[...], dpre_b[...])


def down_grad_kernel(dout_a, dout_b, act_a, act_b, grad_ref):
    grad_ref[...] = dot_lead(act_a[...], dout_a[...]) + dot_lead(act_b[...], dout_b[...])


def shape(dims, kind=bf16):
    return jax.ShapeDtypeStruct(dims, kind)


def params():
    return pltpu.CompilerParams(vmem_limit_bytes=vmem_bytes)


def cost(us):
    return pl.CostEstimate(flops=int(us * 1e9), bytes_accessed=0, transcendentals=0)


smem = pl.BlockSpec(memory_space=pltpu.SMEM)
vmem = pl.BlockSpec(memory_space=pltpu.VMEM)
anywhere = pl.BlockSpec(memory_space=pl.ANY)


def run_forward(second, core, own, other, inputs, slots, experts):
    rows, width = inputs[0].shape
    outs = [shape((rows, width))] * 4 + [
        shape((rows, 128), f32),
        shape((rows, width), f32),
        shape((rows, width)),
        shape((rows, experts), f32),
        shape((rows, 1), f32),
        shape((slots, width)),
    ]
    if second:
        outs += [shape((rows, width)), shape((rows, width)), shape((slots, width))]
    return pl.pallas_call(
        functools.partial(forward_kernel, second),
        out_shape=outs,
        in_specs=[smem] + [anywhere] * (2 * pieces) + [vmem] * len(inputs),
        out_specs=[vmem] * len(outs),
        scratch_shapes=[
            pltpu.VMEM((4, width, width), bf16),
            pltpu.SemaphoreType.DMA((2 * pieces,)),
        ],
        compiler_params=params(),
        cost_estimate=cost(18),
        name="attention_forward",
    )(core, *own, *other, *inputs)


def run_backward(second, core, own, other, inputs, slots, experts, heads):
    rows, width = inputs[0].shape
    outs = [
        shape((rows, width), f32),
        shape((2, width, width)),
        shape((2, width, width)),
        shape((width, experts), f32),
        shape((2, width), f32),
        shape((heads, 2 * rows), f32),
    ]
    if second:
        outs += [shape((rows, width)), shape((slots, width))]
    return pl.pallas_call(
        functools.partial(backward_kernel, second),
        out_shape=outs,
        in_specs=[smem] + [anywhere] * (2 * pieces) + [vmem] * len(inputs),
        out_specs=[vmem] * len(outs),
        scratch_shapes=[pltpu.VMEM((4, width, width), bf16)]
        + [pltpu.VMEM((rows, width), bf16)] * 4
        + [pltpu.VMEM((rows, width), f32), pltpu.SemaphoreType.DMA((2 * pieces,))],
        compiler_params=params(),
        cost_estimate=cost(30),
        name="attention_backward",
    )(core, *own, *other, *inputs)


def run_expert(kernel, mine, tall, middles, ups, downs, n_middle, us, name):
    slots, width = tall.shape
    inner = ups[0].shape[1]
    tiles = 6 if inner % 768 == 0 else 1
    tile = inner // tiles
    whole = pl.BlockSpec((slots, width), lambda j: (0, 0))
    part = pl.BlockSpec((slots, tile), lambda j: (0, j))
    return pl.pallas_call(
        kernel,
        grid=(tiles,),
        out_shape=[shape((slots, inner))] * n_middle + [shape((slots, width))],
        in_specs=[smem, whole] + [part] * len(middles) + [anywhere] * 4,
        out_specs=[part] * n_middle + [whole],
        scratch_shapes=[
            pltpu.VMEM((tiles, width, tile), bf16),
            pltpu.VMEM((tiles, tile, width), bf16),
            pltpu.VMEM((slots, width), f32),
            pltpu.SemaphoreType.DMA((2, tiles)),
        ],
        compiler_params=params(),
        cost_estimate=cost(us),
        name=name,
    )(mine, tall, *middles, *ups, *downs)


def run_up_grad(buf_a, buf_b, dpre_a, dpre_b):
    slots, width = buf_a.shape
    inner = dpre_a.shape[1]
    tile = inner // 6
    whole = pl.BlockSpec((slots, width), lambda j: (0, 0))
    part = pl.BlockSpec((slots, tile), lambda j: (0, j))
    return pl.pallas_call(
        up_grad_kernel,
        grid=(6,),
        out_shape=shape((width, inner), f32),
        in_specs=[whole, whole, part, part],
        out_specs=pl.BlockSpec((width, tile), lambda j: (0, j)),
        compiler_params=params(),
        cost_estimate=cost(10),
        name="up_gradient",
    )(buf_a, buf_b, dpre_a, dpre_b)


def run_down_grad(dout_a, dout_b, act_a, act_b):
    slots, width = dout_a.shape
    inner = act_a.shape[1]
    tile = inner // 6
    whole = pl.BlockSpec((slots, width), lambda j: (0, 0))
    part = pl.BlockSpec((slots, tile), lambda j: (0, j))
    return pl.pallas_call(
        down_grad_kernel,
        grid=(6,),
        out_shape=shape((inner, width), f32),
        in_specs=[whole, whole, part, part],
        out_specs=pl.BlockSpec((tile, width), lambda j: (j, 0)),
        compiler_params=params(),
        cost_estimate=cost(10),
        name="down_gradient",
    )(dout_a, dout_b, act_a, act_b)


def swap(block):
    return lax.ppermute(block, "section", [(0, 1), (1, 0)])


def moved(block, source):
    return lax.ppermute(block, "section", [(source, 1 - source)])


def across(block, bit, devices):
    return lax.ppermute(block, "expert", [(i, i ^ (1 << bit)) for i in range(devices)])


def bit_orders(bits):
    if bits == 4:
        return [(3, 2, 0, 1), (0, 1, 3, 2), (1, 3, 2, 0)]
    names = list(range(bits))
    return [tuple(names[(i + r * bits // pieces) % bits] for i in names) for r in range(pieces)]


def split_lanes(block):
    step = block.shape[-1] // pieces
    return [block[..., p * step : (p + 1) * step] for p in range(pieces)]


def gathered(shard, device, devices):
    bits = devices.bit_length() - 1
    count, rows = shard.shape[:2]
    found = [
        p.reshape((count,) + (1,) * bits + p.shape[1:]) for p in split_lanes(shard)
    ]
    orders = bit_orders(bits)
    for step in range(bits):
        for p in range(pieces):
            bit = orders[p][step]
            axis = bits - bit
            got = across(found[p], bit, devices)
            high = (device >> bit) & 1 == 1
            found[p] = jnp.where(
                high,
                jnp.concatenate([got, found[p]], axis),
                jnp.concatenate([found[p], got], axis),
            )
    return [p.reshape(count, devices * rows, -1) for p in found]


def halved(block, bit, bits, lead, device, devices):
    axis = lead + bits - 1 - bit
    low = lax.index_in_dim(block, 0, axis, keepdims=True)
    high = lax.index_in_dim(block, 1, axis, keepdims=True)
    up = (device >> bit) & 1 == 1
    got = across(jnp.where(up, low, high), bit, devices)
    return jnp.where(up, high, low).astype(f32) + got.astype(f32)


def scattered(total, device, devices):
    bits = devices.bit_length() - 1
    count = total.shape[0]
    found = [
        p.reshape((count,) + (2,) * bits + (total.shape[1] // devices, -1))
        for p in split_lanes(total)
    ]
    orders = [order[::-1] for order in bit_orders(bits)]
    for step in range(bits):
        for p in range(pieces):
            value = halved(found[p], orders[p][step], bits, 1, device, devices)
            found[p] = value if step == bits - 1 else value.astype(bf16)
    return jnp.concatenate([p.reshape(count, total.shape[1] // devices, -1) for p in found], 2)


def body(
    block_input,
    cotangent,
    lengths,
    routes,
    norm_gain,
    attention_in,
    attention_out,
    position_bias,
    router,
    expert_up,
    expert_down,
):
    _, rows, width = block_input.shape
    section = lax.axis_index("section")
    device = lax.axis_index("expert")
    devices = lax.axis_size("expert")
    bits = devices.bit_length() - 1
    first = section == 0
    core = section.astype(jnp.int32).reshape(1)
    mine = [(section == which).astype(jnp.int32).reshape(1) for which in range(2)]
    experts = router.shape[2]
    shard_rows = router.shape[1]
    buckets, heads = position_bias.shape[1:]
    capacity = max(2, 3 * rows // (2 * experts))
    capacity = -(-capacity // 8) * 8
    slots = experts * capacity

    def both(own, other):
        return (jnp.where(first, own, other), jnp.where(first, other, own))

    def own_micro(block):
        return jnp.where(first, block[0], block[1])

    def other_micro(block):
        return jnp.where(first, block[1], block[0])

    queries_keys = attention_in[0, :2]
    values_out = jnp.stack([attention_in[0, 2], attention_out[0]])
    given = swap(jnp.where(first, values_out, queries_keys))
    shards = (
        jnp.where(first, queries_keys, given),
        jnp.where(first, given, values_out),
    )
    small_parts = (
        norm_gain[0].reshape(-1),
        position_bias[0].reshape(-1),
        router[0].astype(f32).reshape(-1),
        other_micro(routes[0])[:, 0].astype(f32),
    )
    small = jnp.concatenate(small_parts).reshape(-1, 128)
    small_given = swap(small).reshape(-1)
    split_at, at = [], 0
    for part in small_parts[:-1]:
        at += part.shape[0]
        split_at.append(at)
    gain_other, table_other, router_other, route_other = jnp.split(small_given, split_at)
    gains = both(norm_gain[0], gain_other.reshape(2, width))
    tables = both(position_bias[0], table_other.reshape(buckets, heads))
    route_pair = both(own_micro(routes[0])[:, 0], route_other.astype(jnp.int32))
    router_pair = both(router[0], router_other.reshape(shard_rows, experts).astype(bf16))

    first_weights = gathered(shards[0], device, devices)
    first_other = [swap(p) for p in first_weights]
    up_other = swap(expert_up[0, 0])
    down_other = swap(expert_down[0, 0])

    routers = jnp.concatenate(router_pair, axis=1)
    routers = jnp.pad(routers, ((0, 0), (0, -routers.shape[1] % 128)))
    routers = routers.reshape((1,) * bits + routers.shape)
    for bit in range(bits):
        axis = bits - 1 - bit
        got = across(routers, bit, devices)
        routers = jnp.where(
            (device >> bit) & 1 == 1,
            jnp.concatenate([got, routers], axis),
            jnp.concatenate([routers, got], axis),
        )
    routers = routers.reshape(width, -1)
    router_all = (routers[:, :experts], routers[:, experts : 2 * experts])

    late, first_weights = lax.optimization_barrier((shards[1], first_weights))
    second_weights = gathered(late, device, devices)
    second_other = [swap(p) for p in second_weights]
    owns, others = (first_weights, second_weights), (first_other, second_other)

    positions = jnp.arange(rows, dtype=jnp.int32)
    bounds = jnp.cumsum(own_micro(lengths)[0])
    segment = jnp.sum((positions[:, None] >= bounds[None, :]).astype(jnp.int32), axis=1)
    seg_col, seg_row = segment[:, None], segment[None, :]
    offsets = jnp.arange(2 * rows, dtype=jnp.int32) - (rows - 1)
    bucket_hot = (
        bucket_of(offsets)[:, None] == jnp.arange(buckets, dtype=jnp.int32)[None, :]
    ).astype(f32)
    lines = [
        lax.dot_general(table, bucket_hot, (((0,), (1,)), ((), ())), precision=highest)
        for table in tables
    ]
    before = (positions[:, None] > positions[None, :]).astype(bf16)
    places = []
    for route in route_pair:
        chosen = route[:, None] == jnp.arange(experts, dtype=jnp.int32)[None, :]
        earlier = dot(before, chosen.astype(bf16))
        slot = jnp.sum(jnp.where(chosen, earlier, 0.0), axis=1).astype(jnp.int32)
        places.append(route * capacity + slot)
    route_cols = [route[:, None] for route in route_pair]
    place_cols = [place[:, None] for place in places]
    place_rows = [place[None, :] for place in places]
    ups, downs = (expert_up[0, 0], up_other), (expert_down[0, 0], down_other)

    def exchanged(block):
        return lax.all_to_all(block, "expert", split_axis=0, concat_axis=0, tiled=True)

    def expert_forward(which, arrived):
        return run_expert(
            expert_forward_kernel, mine[which], arrived, (), ups, downs, 2, 11, "expert_forward"
        )

    def expert_backward(which, arrived, slope):
        return run_expert(
            expert_backward_kernel, mine[which], arrived, (slope,), ups, downs, 1, 11,
            "expert_backward",
        )

    def shared_inputs(which):
        return (
            gains[which], router_all[which], lines[which], seg_col, seg_row, route_cols[which],
        )

    inputs = own_micro(block_input)
    cot = own_micro(cotangent)
    q0, k0, v0, o0, lse0, mid0, h20, share0, gate0, send0 = run_forward(
        False, core, owns[0], others[0], (inputs, *shared_inputs(0), place_rows[0]), slots, experts
    )
    buf0 = exchanged(send0)
    act0, slope0, result0 = expert_forward(0, buf0)
    back0 = exchanged(result0)
    q1, k1, v1, o1, lse1, mid1, h21, share1, gate1, send1, between, combined0, grad_send1 = (
        run_forward(
            True, core, owns[1], others[1],
            (mid0, gate0, place_cols[0], back0, cot, *shared_inputs(1), place_rows[1]),
            slots, experts,
        )
    )
    buf1 = exchanged(send1)
    grad_send1, _ = lax.optimization_barrier((grad_send1, buf1))
    dout1 = exchanged(grad_send1)
    act1, slope1, result1 = expert_forward(1, buf1)
    back1 = exchanged(result1)
    dpre1, dbuf1 = expert_backward(1, dout1, slope1)
    dback1 = exchanged(dbuf1)
    dx1, keep1, give1, router_grad1, gain_grad1, line_grad1, last, grad_send0 = run_backward(
        True, core, owns[1], others[1],
        (between, q1, k1, v1, o1, lse1, mid1, h21, share1, gate1, cot, dback1, back1,
         *shared_inputs(1), place_cols[1], gate0, place_rows[0]),
        slots, experts, heads,
    )
    dout0 = exchanged(grad_send0)
    dpre0, dbuf0 = expert_backward(0, dout0, slope0)
    dback0 = exchanged(dbuf0)
    dx0, keep0, give0, router_grad0, gain_grad0, line_grad0 = run_backward(
        False, core, owns[0], others[0],
        (inputs, q0, k0, v0, o0, lse0, mid0, h20, share0, gate0, dx1.astype(bf16), dback0,
         combined0, *shared_inputs(0), place_cols[0]),
        slots, experts, heads,
    )

    from_first = [moved(block, 0) for block in (buf1, act1, dout1, dpre1)]
    from_second = [moved(block, 1) for block in (buf0, act0, dout0, dpre0)]

    def up_of(bufs, dpres):
        return run_up_grad(*bufs, *dpres)

    def down_of(douts, acts):
        return run_down_grad(*douts, *acts)

    first_sets = ((buf0, from_second[0]), (dpre0, from_second[3]))
    second_sets = ((buf1, from_first[0]), (dpre1, from_first[3]))
    grad_up = lax.cond(
        first, lambda a, b: up_of(*a), lambda a, b: up_of(*b), first_sets, second_sets
    )
    first_sets = ((dout0, from_second[2]), (act0, from_second[1]))
    second_sets = ((dout1, from_first[2]), (act1, from_first[1]))
    grad_down = lax.cond(
        first, lambda a, b: down_of(*a), lambda a, b: down_of(*b), first_sets, second_sets
    )

    def reduced(keep, give):
        total = (keep.astype(f32) + swap(give).astype(f32)).astype(bf16)
        return scattered(total, device, devices)

    shared1 = reduced(keep1, give1)
    shared0 = reduced(keep0, give0)
    shared_other = swap(jnp.where(first, shared1, shared0))
    queries_keys = jnp.where(first, shared0, shared_other)
    values_out = jnp.where(first, shared_other, shared1)

    router_mine = jnp.where(first, router_grad0, router_grad1)
    router_given = jnp.where(first, router_grad1, router_grad0)
    router_sum = (router_mine + swap(router_given)).reshape((2,) * bits + (shard_rows, experts))
    little = [
        jnp.concatenate([gain, line], axis=0)
        for gain, line in ((gain_grad0, line_grad0), (gain_grad1, line_grad1))
    ]
    little_sum = jnp.where(first, little[0], little[1]) + swap(
        jnp.where(first, little[1], little[0])
    )
    for bit in range(bits):
        router_sum = halved(router_sum, bit, bits, 0, device, devices)
        little_sum = little_sum + across(little_sum, bit, devices)
    grad_table = jnp.dot(little_sum[2:], bucket_hot, precision=highest).T

    out_other = swap(jnp.where(first, last, between))
    layer_out = jnp.stack(
        [jnp.where(first, between, out_other), jnp.where(first, out_other, last)]
    )
    grad_other = swap(jnp.where(first, dx1, dx0))
    input_grad = jnp.stack([jnp.where(first, dx0, grad_other), jnp.where(first, grad_other, dx1)])
    return (
        layer_out[None],
        input_grad[None],
        little_sum[:2][None],
        jnp.concatenate([queries_keys, values_out[:1]], axis=0)[None],
        values_out[1][None],
        grad_table[None],
        router_sum.reshape(1, shard_rows, experts),
        grad_up[None, None],
        grad_down[None, None],
    )


def solution(mesh):
    in_specs = (
        P(None, "expert", None),
        P(None, "expert", None),
        P(None, "expert", None),
        P("section", None, "expert", None),
        P("section", None, None),
        P("section", None, "expert", None),
        P("section", "expert", None),
        P("section", None, None),
        P("section", "expert", None),
        P("section", "expert", None, None),
        P("section", "expert", None, None),
    )
    out_specs = (
        P("section", None, "expert", None),
        P("section", None, "expert", None),
        P("section", None, None),
        P("section", None, "expert", None),
        P("section", "expert", None),
        P("section", None, None),
        P("section", "expert", None),
        P("section", "expert", None, None),
        P("section", "expert", None, None),
    )
    return jax.shard_map(body, mesh=mesh, in_specs=in_specs, out_specs=out_specs, check_vma=False)
```

```python
import functools

import jax
import jax.numpy as jnp
from jax import lax
from jax.experimental import pallas as pl
from jax.experimental.pallas import tpu as pltpu
from jax.sharding import PartitionSpec as P

bucket_edges = (12, 16, 23, 32, 46, 64, 91)
norm_eps = 1e-06
gelu_c = 0.7978845608028654
gelu_cube = 0.044715
masked_score = -1e30
highest = lax.Precision.HIGHEST
f32 = jnp.float32
bf16 = jnp.bfloat16
vmem_bytes = 56 * 2**20
pieces = 3


def dot(left, right):
    return jnp.dot(left, right, preferred_element_type=f32)


def dot_lead(left, right):
    return lax.dot_general(left, right, (((0,), (0,)), ((), ())), preferred_element_type=f32)


def dot_last(left, right):
    return lax.dot_general(left, right, (((1,), (1,)), ((), ())), preferred_element_type=f32)


def gelu_pair(value):
    square = value * value
    inner = jnp.tanh(gelu_c * value * (1.0 + gelu_cube * square))
    half = 0.5 * (1.0 + inner)
    slope = half + 0.5 * value * (1.0 - inner * inner) * (
        gelu_c * (1.0 + 3.0 * gelu_cube * square)
    )
    return (value * half, slope)


def bucket_of(offset):
    distance = jnp.abs(offset)
    found = 16 * (offset > 0).astype(jnp.int32) + jnp.minimum(distance, 8)
    for edge in bucket_edges:
        found = found + (distance >= edge).astype(jnp.int32)
    return found


def norm_scale(values):
    return lax.rsqrt(jnp.mean(values * values, axis=-1, keepdims=True) + norm_eps)


def norm_backward(values, gain, grad_normed):
    scale = norm_scale(values)
    normal = values * scale
    inner = grad_normed * gain
    grad_values = scale * (inner - normal * jnp.mean(inner * normal, axis=-1, keepdims=True))
    return (grad_values, jnp.sum(grad_normed * normal, axis=0, keepdims=True))


def zero_token(token_ref):
    token_ref[0] = 0


def weight_copies(place_ref, layer, matrices, blocks, weights, router, sems):
    core, device = place_ref[0], place_ref[1]
    first, count = matrices
    copies = []
    for p in range(pieces):
        for (here, differ), (there, _) in zip(blocks[0][p], blocks[1][p]):
            rows, step = here.shape[2:]
            for at in range(here.shape[0]):
                target = pl.ds(pl.multiple_of((device ^ differ[at]) * rows, rows), rows)
                couples = [
                    (pl.ds(first, count), pl.ds(0, step), weights.at[:, target, pl.ds(p * step, step)])
                ]
                if p == 0 and router is not None:
                    couples.append((4, pl.ds(0, 128), router.at[target, :]))
                for which, lanes, goal in couples:
                    sem = sems.at[len(copies)]
                    own = pltpu.make_async_copy(here.at[at, which, :, lanes], goal, sem)
                    other = pltpu.make_async_copy(there.at[at, which, :, lanes], goal, sem)
                    copies.append(own)
                    pl.when(core == layer)(own.start)
                    pl.when(core != layer)(other.start)
    return copies


def laid_out(layout, refs):
    blocks, at = [], 0
    for _ in range(2):
        blocks.append([])
        for piece in layout:
            blocks[-1].append([(refs[at + i], differ) for i, differ in enumerate(piece)])
            at += len(piece)
    return blocks, refs[at:]


def join_kernel(place_ref, *refs):
    olds, gots, outs = refs[:pieces], refs[pieces : 2 * pieces], refs[2 * pieces :]
    token_ref, outs = outs[0], outs[1:]
    zero_token(token_ref)
    for old, got, out in zip(olds, gots, outs):
        half = old.shape[0]
        out[:half] = old[...]
        out[half:] = got[...]


def head_masks():
    lane = lax.broadcasted_iota(jnp.int32, (1, 128), 1)
    low = (lane < 64).astype(f32)
    return (low.astype(bf16), (1.0 - low).astype(bf16))


def bias_kernel(line_ref, base_ref):
    heads, _, reach = base_ref.shape
    wide = line_ref.shape[1]

    def one(head, carry):
        line = jnp.broadcast_to(line_ref[pl.ds(head, 1), :], (128, wide))
        turned = pltpu.roll(line, wide - 127, 1, stride=1, stride_axis=0)
        base_ref[head] = turned[:, :reach]
        return carry

    lax.fori_loop(0, heads, one, 0)


def bias_of(base_ref, head, rows):
    blocks = rows // 128
    return jnp.concatenate(
        [base_ref[head, :, 128 * (blocks - 1 - a) : 128 * (blocks - 1 - a) + rows] for a in range(blocks)],
        axis=0,
    )


def diagonal_line(grad_scores, flip, wide):
    blocks = grad_scores.shape[0] // 128
    parts = [None] * (wide // 128)
    for a in range(blocks):
        flipped = dot(flip, grad_scores[128 * a : 128 * (a + 1), :])
        for j in range(blocks):
            piece = flipped[:, 128 * j : 128 * (j + 1)]
            at = j + blocks - 1 - a
            parts[at] = piece if parts[at] is None else parts[at] + piece
    empty = jnp.zeros((128, 128), f32)
    sums = jnp.concatenate([empty if part is None else part for part in parts], axis=1)
    turned = pltpu.roll(sums, 0, 1, stride=1, stride_axis=0)
    return jnp.sum(turned, axis=0, keepdims=True)


def one_hot_columns(place_col, slots):
    rows = place_col.shape[0]
    return (place_col == lax.broadcasted_iota(jnp.int32, (rows, slots), 1)).astype(f32).astype(bf16)


def one_hot_rows(place_row, slots):
    rows = place_row.shape[1]
    return (place_row == lax.broadcasted_iota(jnp.int32, (slots, rows), 0)).astype(f32).astype(bf16)


def forward_kernel(second, experts, layout, core_ref, *refs):
    blocks, refs = laid_out(layout, refs)
    if second:
        (before_ref, gate_before_ref, place_before_ref, back_ref, cot_ref), refs = refs[:5], refs[5:]
    else:
        (x_ref,), refs = refs[:1], refs[1:]
    (gain_ref, base_ref, seg_col_ref, seg_row_ref, route_ref, place_ref), refs = (
        refs[:6],
        refs[6:],
    )
    (
        token_ref, q_ref, k_ref, v_ref, o_ref, p_ref, mid_ref, h2_ref, share_ref, gate_ref, send_ref,
    ), refs = refs[:11], refs[11:]
    if second:
        (x_out_ref, combined_ref, grad_send_ref), refs = refs[:3], refs[3:]
    weights, router_ref, mask_ref, sems = refs
    zero_token(token_ref)
    copies = weight_copies(core_ref, int(second), (0, 4), blocks, weights, router_ref, sems)
    slots = send_ref.shape[0]
    rows = q_ref.shape[0]
    if second:
        scatter = one_hot_columns(place_before_ref[...], slots)
        combined = dot(scatter, back_ref[...])
        combined_ref[...] = combined.astype(bf16)
        low = (before_ref[...] + gate_before_ref[...] * combined).astype(bf16)
        x_out_ref[...] = low
        wide = low.astype(f32)
    else:
        wide = x_ref[...].astype(f32)
    h1 = (wide * norm_scale(wide) * gain_ref[0:1, :]).astype(bf16)
    mask_ref[...] = jnp.where(seg_col_ref[...] == seg_row_ref[...], 0.0, masked_score)
    for copy in copies:
        copy.wait()
    q_ref[...] = dot(h1, weights[0]).astype(bf16)
    k_ref[...] = dot(h1, weights[1]).astype(bf16)
    v_ref[...] = dot(h1, weights[2]).astype(bf16)
    masks = head_masks()

    def pair(p, carry):
        columns = pl.ds(pl.multiple_of(p * 128, 128), 128)
        queries, keys, values = q_ref[:, columns], k_ref[:, columns], v_ref[:, columns]
        mixed = jnp.zeros((rows, 128), f32)
        for half in range(2):
            head = 2 * p + half
            scores = dot_last(queries * masks[half], keys) * 0.125 + bias_of(base_ref, head, rows)
            scores = scores + mask_ref[...]
            raised = jnp.exp(scores - jnp.max(scores, axis=-1, keepdims=True))
            total = jnp.sum(raised, axis=-1, keepdims=True)
            shares = (raised * (1.0 / total)).astype(bf16)
            p_ref[head] = shares
            mixed = mixed + dot(shares, values * masks[half])
        o_ref[:, columns] = mixed.astype(bf16)
        return carry

    lax.fori_loop(0, p_ref.shape[0] // 2, pair, 0)
    middle = wide + dot(o_ref[...], weights[3])
    mid_ref[...] = middle
    h2 = (middle * norm_scale(middle) * gain_ref[1:2, :]).astype(bf16)
    h2_ref[...] = h2
    logits = dot(h2, router_ref[...])
    lane = lax.broadcasted_iota(jnp.int32, (1, 128), 1)
    logits = jnp.where(lane < experts, logits, masked_score)
    raised = jnp.exp(logits - jnp.max(logits, axis=-1, keepdims=True))
    shares = raised / jnp.sum(raised, axis=-1, keepdims=True)
    share_ref[...] = shares
    chosen = route_ref[...] == lax.broadcasted_iota(jnp.int32, shares.shape, 1)
    gate = jnp.sum(jnp.where(chosen, shares, 0.0), axis=-1, keepdims=True)
    gate_ref[...] = gate
    gather = one_hot_rows(place_ref[...], slots)
    send_ref[...] = dot(gather, h2).astype(bf16)
    if second:
        grad_out = (gate * cot_ref[...].astype(f32)).astype(bf16)
        grad_send_ref[...] = dot(gather, grad_out).astype(bf16)


def heads_backward_kernel(second, layout, core_ref, *refs):
    blocks, refs = laid_out(layout, refs)
    (
        q_ref, k_ref, v_ref, p_ref, mid_ref, h2_ref, share_ref, gate_ref, dy_ref, dback_ref,
        out_ref, gain_ref, route_ref, place_ref,
    ), refs = refs[:14], refs[14:]
    (
        token_ref, dx1_ref, low_ref, dq_ref, dk_ref, dv_ref, router_grad_ref, gain_grad_ref,
        line_grad_ref,
    ), refs = refs[:9], refs[9:]
    if second:
        (y_ref,), refs = refs[:1], refs[1:]
    weights, router_ref, do_ref, sems = refs
    zero_token(token_ref)
    copies = weight_copies(core_ref, int(second), (3, 1), blocks, weights, router_ref, sems)
    rows = q_ref.shape[0]
    slots = dback_ref.shape[0]
    dy = dy_ref[...].astype(f32)
    gate = gate_ref[...]
    middle = mid_ref[...]
    scatter = one_hot_columns(place_ref[...], slots)
    if second:
        combined = dot(one_hot_columns(out_ref[...], slots), dback_ref[...])
        y_ref[...] = (middle + gate * combined).astype(bf16)
    else:
        combined = out_ref[...].astype(f32)
    grad_gate = jnp.sum(dy * combined, axis=-1, keepdims=True)
    shares = share_ref[...]
    chosen = route_ref[...] == lax.broadcasted_iota(jnp.int32, shares.shape, 1)
    grad_logits = (grad_gate * gate * (chosen.astype(f32) - shares)).astype(bf16)
    router_grad_ref[...] = dot_lead(grad_logits, h2_ref[...])[: router_grad_ref.shape[0]]
    for copy in copies:
        copy.wait()
    grad_two = dot(scatter, dback_ref[...]) + dot_last(grad_logits, router_ref[...])
    grad_middle, gain_two = norm_backward(middle, gain_ref[1:2, :], grad_two)
    gain_grad_ref[...] = gain_two
    grad_middle = grad_middle + dy
    dx1_ref[...] = grad_middle
    low = grad_middle.astype(bf16)
    low_ref[...] = low
    do_ref[...] = dot_last(low, weights[0]).astype(bf16)
    masks = head_masks()
    flip = (
        lax.broadcasted_iota(jnp.int32, (128, 128), 0)
        + lax.broadcasted_iota(jnp.int32, (128, 128), 1)
        == 127
    )
    flip = flip.astype(f32).astype(bf16)

    def pair(p, carry):
        columns = pl.ds(pl.multiple_of(p * 128, 128), 128)
        queries, keys, values = q_ref[:, columns], k_ref[:, columns], v_ref[:, columns]
        grad_mixed = do_ref[:, columns]
        dq = jnp.zeros((rows, 128), f32)
        dk = jnp.zeros((rows, 128), f32)
        dv = jnp.zeros((rows, 128), f32)
        for half in range(2):
            head = 2 * p + half
            own_mixed = grad_mixed * masks[half]
            low_shares = p_ref[head]
            shares = low_shares.astype(f32)
            grad_shares = dot_last(own_mixed, values)
            mean = jnp.sum(shares * grad_shares, axis=-1, keepdims=True)
            grad_scores = (shares * (grad_shares - mean)).astype(bf16)
            dv = dv + dot_lead(low_shares, own_mixed)
            dq = dq + dot(grad_scores, keys * masks[half])
            dk = dk + dot_lead(grad_scores, queries * masks[half])
            line_grad_ref[pl.ds(head, 1), :] = diagonal_line(
                grad_scores, flip, line_grad_ref.shape[1]
            )
        dq_ref[:, columns] = (dq * 0.125).astype(bf16)
        dk_ref[:, columns] = (dk * 0.125).astype(bf16)
        dv_ref[:, columns] = dv.astype(bf16)
        return carry

    lax.fori_loop(0, p_ref.shape[0] // 2, pair, 0)


def input_backward_kernel(second, layout, core_ref, *refs):
    blocks, refs = laid_out(layout, refs)
    (x_ref, dx1_ref, dq_ref, dk_ref, dv_ref, gain_ref), refs = refs[:6], refs[6:]
    if second:
        (gate_next_ref, place_next_ref), refs = refs[:2], refs[2:]
    (token_ref, dx_ref, gain_grad_ref), refs = refs[:3], refs[3:]
    if second:
        (low_out_ref, grad_send_ref), refs = refs[:2], refs[2:]
    weights, sems = refs
    zero_token(token_ref)
    copies = weight_copies(core_ref, int(second), (0, 3), blocks, weights, None, sems)
    for copy in copies:
        copy.wait()
    wide = x_ref[...].astype(f32)
    grad_one = (
        dot_last(dq_ref[...], weights[0])
        + dot_last(dk_ref[...], weights[1])
        + dot_last(dv_ref[...], weights[2])
    )
    grad_inputs, gain_one = norm_backward(wide, gain_ref[0:1, :], grad_one)
    grad_inputs = grad_inputs + dx1_ref[...]
    dx_ref[...] = grad_inputs
    gain_grad_ref[...] = gain_one
    if second:
        low = grad_inputs.astype(bf16)
        low_out_ref[...] = low
        grad_out = (gate_next_ref[...] * low.astype(f32)).astype(bf16)
        gather = one_hot_rows(place_next_ref[...], grad_send_ref.shape[0])
        grad_send_ref[...] = dot(gather, grad_out).astype(bf16)


def weight_backward_kernel(core_ref, x_ref, gain_ref, o_ref, low_ref, dq_ref, dk_ref, dv_ref, *refs):
    token_ref, keep_ref, give_ref = refs
    zero_token(token_ref)
    core = core_ref[0]

    def put(matrix, value):
        value = value.astype(bf16)

        @pl.when(core == matrix // 2)
        def _():
            keep_ref[matrix % 2] = value

        @pl.when(core != matrix // 2)
        def _():
            give_ref[matrix % 2] = value

    wide = x_ref[...].astype(f32)
    h1 = (wide * norm_scale(wide) * gain_ref[0:1, :]).astype(bf16)
    put(0, dot_lead(h1, dq_ref[...]))
    put(1, dot_lead(h1, dk_ref[...]))
    put(2, dot_lead(h1, dv_ref[...]))
    put(3, dot_lead(o_ref[...], low_ref[...]))


def places_of(block, order):
    place = 0
    for bit in order:
        place = 2 * place + ((block >> bit) & 1)
    return place


def fold_first_kernel(orders, device_ref, *refs):
    sums, outs = refs[:4], refs[4:]
    token_ref, outs = outs[0], outs[1:]
    zero_token(token_ref)
    keeps, sends = outs[:pieces], outs[pieces:]
    device = device_ref[0]
    half, rows, step = keeps[0].shape[1:]
    for block in range(2 * half):
        at = pl.ds(pl.multiple_of((device ^ block) * rows, rows), rows)
        for layer in range(2):
            for matrix in range(2):
                total = sums[2 * layer][matrix, at, :].astype(f32)
                total = (total + sums[2 * layer + 1][matrix, at, :].astype(f32)).astype(bf16)
                for p in range(pieces):
                    place = places_of(block, orders[p])
                    target = sends[p] if place >= half else keeps[p]
                    target[2 * layer + matrix, place % half] = total[:, p * step : (p + 1) * step]


def fold_kernel(device_ref, *refs):
    olds, gots, outs = refs[:pieces], refs[pieces : 2 * pieces], refs[2 * pieces :]
    token_ref, outs = outs[0], outs[1:]
    zero_token(token_ref)
    for p in range(pieces):
        total = olds[p][...].astype(f32) + gots[p][...].astype(f32)
        half = total.shape[1] // 2
        outs[p][...] = total[:, :half].astype(bf16)
        outs[pieces + p][...] = total[:, half:].astype(bf16)


def fold_last_kernel(device_ref, *refs):
    olds, gots, (token_ref, out_ref) = refs[:pieces], refs[pieces : 2 * pieces], refs[2 * pieces :]
    zero_token(token_ref)
    for p in range(pieces):
        step = olds[p].shape[3]
        total = olds[p][...].astype(f32) + gots[p][...].astype(f32)
        out_ref[:, :, p * step : (p + 1) * step] = total[:, 0]


def expert_copies(mine, tiles, up_refs, down_refs, up, down, sems, start):
    width = up.shape[2]

    def copies(which):
        found = []
        for j in range(tiles):
            at = pl.ds(j * width, width)
            found.append(
                (
                    pltpu.make_async_copy(up_refs[which].at[:, at], up.at[j], sems.at[0, j]),
                    pltpu.make_async_copy(down_refs[which].at[at, :], down.at[j], sems.at[1, j]),
                )
            )
        return found

    if start:
        for which in range(2):

            @pl.when(mine == 1 - which)
            def _():
                for couple in copies(which):
                    for copy in couple:
                        copy.start()


def expert_wait(j, up_ref, down_ref, up, down, sems):
    width = up.shape[2]
    at = pl.ds(0, width)
    pltpu.make_async_copy(up_ref.at[:, at], up.at[j], sems.at[0, j]).wait()
    pltpu.make_async_copy(down_ref.at[at, :], down.at[j], sems.at[1, j]).wait()


def expert_forward_kernel(
    mine_ref, x_ref, up_own, up_other, down_own, down_other, act_ref, slope_ref, out_ref,
    up, down, total, sems,
):
    j = pl.program_id(0)
    tiles = up.shape[0]

    @pl.when(j == 0)
    def _():
        expert_copies(
            mine_ref[0], tiles, (up_own, up_other), (down_own, down_other), up, down, sems, True
        )
        total[...] = jnp.zeros_like(total)

    expert_wait(j, up_own, down_own, up, down, sems)
    active, slope = gelu_pair(dot(x_ref[...], up[j]))
    active = active.astype(bf16)
    act_ref[...] = active
    slope_ref[...] = slope.astype(bf16)
    total[...] += dot(active, down[j])

    @pl.when(j == tiles - 1)
    def _():
        out_ref[...] = total[...].astype(bf16)


def expert_backward_kernel(
    mine_ref, dout_ref, slope_ref, up_own, up_other, down_own, down_other, dpre_ref, dbuf_ref,
    up, down, total, sems,
):
    j = pl.program_id(0)
    tiles = up.shape[0]

    @pl.when(j == 0)
    def _():
        expert_copies(
            mine_ref[0], tiles, (up_own, up_other), (down_own, down_other), up, down, sems, True
        )
        total[...] = jnp.zeros_like(total)

    expert_wait(j, up_own, down_own, up, down, sems)
    grad_pre = (dot_last(dout_ref[...], down[j]) * slope_ref[...].astype(f32)).astype(bf16)
    dpre_ref[...] = grad_pre
    total[...] += dot_last(grad_pre, up[j])

    @pl.when(j == tiles - 1)
    def _():
        dbuf_ref[...] = total[...].astype(bf16)


def up_grad_kernel(buf_a, buf_b, dpre_a, dpre_b, grad_ref):
    grad_ref[...] = dot_lead(buf_a[...], dpre_a[...]) + dot_lead(buf_b[...], dpre_b[...])


def down_grad_kernel(dout_a, dout_b, act_a, act_b, grad_ref):
    grad_ref[...] = dot_lead(act_a[...], dout_a[...]) + dot_lead(act_b[...], dout_b[...])


def shape(dims, kind=bf16):
    return jax.ShapeDtypeStruct(dims, kind)


def params():
    return pltpu.CompilerParams(vmem_limit_bytes=vmem_bytes)


def cost(us):
    return pl.CostEstimate(flops=int(us * 1e9), bytes_accessed=0, transcendentals=0)


smem = pl.BlockSpec(memory_space=pltpu.SMEM)
vmem = pl.BlockSpec(memory_space=pltpu.VMEM)
anywhere = pl.BlockSpec(memory_space=pl.ANY)


def run(kernel, name, us, inputs, outs, scratch, core, weights=(), after=()):
    def marked(core_ref, *refs):
        at = len(weights) + len(inputs)
        return kernel(core_ref, *refs[:at], *refs[at + len(after) :])

    outs = [shape((1,), jnp.int32)] + list(outs)
    return pl.pallas_call(
        marked,
        out_shape=outs,
        in_specs=[smem]
        + [anywhere] * len(weights)
        + [vmem] * len(inputs)
        + [anywhere] * len(after),
        out_specs=[smem] + [vmem] * (len(outs) - 1),
        scratch_shapes=scratch,
        compiler_params=params(),
        cost_estimate=cost(us),
        name=name,
    )(core, *weights, *inputs, *after)


def weight_scratch(layout, count, width, router):
    copies = sum(len(differ) for piece in layout for differ in piece)
    held = [pltpu.VMEM((count, width, width), bf16)]
    if router:
        copies += sum(len(differ) for differ in layout[0])
        held.append(pltpu.VMEM((width, 128), bf16))
    return held, [pltpu.SemaphoreType.DMA((copies,))]


def run_bias(line, rows):
    heads, wide = line.shape
    return pl.pallas_call(
        bias_kernel,
        out_shape=shape((heads, 128, 2 * rows - 128), f32),
        in_specs=[vmem],
        out_specs=vmem,
        compiler_params=params(),
        cost_estimate=cost(3),
        name="bias_base",
    )(line)


def run_forward(second, layout, core, weights, inputs, slots, experts, heads, after):
    rows, width = inputs[0].shape
    outs = [shape((rows, width))] * 4 + [
        shape((heads, rows, rows)),
        shape((rows, width), f32),
        shape((rows, width)),
        shape((rows, 128), f32),
        shape((rows, 1), f32),
        shape((slots, width)),
    ]
    if second:
        outs += [shape((rows, width)), shape((rows, width)), shape((slots, width))]
    held, sems = weight_scratch(layout, 4, width, True)
    return run(
        functools.partial(forward_kernel, second, experts, layout), "attention_forward", 15, inputs, outs,
        held + [pltpu.VMEM((rows, rows), f32)] + sems, core, weights, after,
    )


def run_heads_backward(second, layout, core, weights, inputs, experts, after):
    rows, width = inputs[0].shape
    heads = inputs[3].shape[0]
    outs = [shape((rows, width), f32)] + [shape((rows, width))] * 4 + [
        shape((experts, width), f32),
        shape((1, width), f32),
        shape((heads, 2 * rows), f32),
    ]
    if second:
        outs += [shape((rows, width))]
    held, sems = weight_scratch(layout, 1, width, True)
    return run(
        functools.partial(heads_backward_kernel, second, layout), "heads_backward", 20, inputs, outs,
        held + [pltpu.VMEM((rows, width), bf16)] + sems, core, weights, after,
    )


def run_input_backward(second, layout, core, weights, inputs, slots, after):
    rows, width = inputs[0].shape
    outs = [shape((rows, width), f32), shape((1, width), f32)]
    if second:
        outs += [shape((rows, width)), shape((slots, width))]
    held, sems = weight_scratch(layout, 3, width, False)
    return run(
        functools.partial(input_backward_kernel, second, layout), "input_backward", 6, inputs, outs,
        held + sems, core, weights, after,
    )


def run_weight_backward(core, inputs, after):
    width = inputs[0].shape[1]
    outs = [shape((2, width, width))] * 2
    return run(weight_backward_kernel, "weight_backward", 6, inputs, outs, [], core, (), after)


def summed_blocks(pairs, little, device, devices, beside, after):
    bits = devices.bit_length() - 1
    _, tall, width = pairs[0].shape
    rows, step = tall // devices, width // pieces
    orders = [order[::-1] for order in bit_orders(bits)]
    me = device.astype(jnp.int32).reshape(1)
    if rows % 16:
        found = unfolded(
            jnp.concatenate(
                [(pairs[i].astype(f32) + pairs[i + 1].astype(f32)).astype(bf16) for i in (0, 2)]
            ),
            devices,
        )
        for at in range(bits):
            found = folded(found, at, device, devices)
            little = little + across(little, at, devices)
        sums = jnp.concatenate([p.reshape(4, rows, -1) for p in found], 2)
        return sums, little, [call(0) for call in beside]
    half = devices // 2
    outs = [shape((4, half, rows, step))] * (2 * pieces)
    found = run(
        functools.partial(fold_first_kernel, orders), "fold_first", 4, pairs, outs, [], me, (), after
    )
    results = []
    for at in range(bits):
        token, found = found[0], found[1:]
        after = ()
        if at < len(beside):
            after = (beside[at](token[0]),)
            results.extend(after)
        keeps = found[:pieces]
        gots = [across(found[pieces + p], orders[p][at], devices) for p in range(pieces)]
        little = little + token.astype(f32)
        little = little + across(little, at, devices)
        half //= 2
        if half:
            outs = [shape((4, half, rows, step))] * (2 * pieces)
            found = run(fold_kernel, "fold", 2, [*keeps, *gots], outs, [], me, (), after)
        else:
            outs = [shape((4, rows, width), f32)]
            found = run(fold_last_kernel, "fold_last", 1, [*keeps, *gots], outs, [], me)
    return found[1], little, results


def run_expert(kernel, mine, tall, middles, ups, downs, n_middle, us, name):
    slots, width = tall.shape
    inner = ups[0].shape[1]
    tiles = 6 if inner % 768 == 0 else 1
    tile = inner // tiles
    whole = pl.BlockSpec((slots, width), lambda j: (0, 0))
    part = pl.BlockSpec((slots, tile), lambda j: (0, j))
    return pl.pallas_call(
        kernel,
        grid=(tiles,),
        out_shape=[shape((slots, inner))] * n_middle + [shape((slots, width))],
        in_specs=[smem, whole] + [part] * len(middles) + [anywhere] * 4,
        out_specs=[part] * n_middle + [whole],
        scratch_shapes=[
            pltpu.VMEM((tiles, width, tile), bf16),
            pltpu.VMEM((tiles, tile, width), bf16),
            pltpu.VMEM((slots, width), f32),
            pltpu.SemaphoreType.DMA((2, tiles)),
        ],
        compiler_params=params(),
        cost_estimate=cost(us),
        name=name,
    )(mine, tall, *middles, *ups, *downs)


def run_up_grad(buf_a, buf_b, dpre_a, dpre_b):
    slots, width = buf_a.shape
    inner = dpre_a.shape[1]
    tile = inner // 6
    whole = pl.BlockSpec((slots, width), lambda j: (0, 0))
    part = pl.BlockSpec((slots, tile), lambda j: (0, j))
    return pl.pallas_call(
        up_grad_kernel,
        grid=(6,),
        out_shape=shape((width, inner), f32),
        in_specs=[whole, whole, part, part],
        out_specs=pl.BlockSpec((width, tile), lambda j: (0, j)),
        compiler_params=params(),
        cost_estimate=cost(10),
        name="up_gradient",
    )(buf_a, buf_b, dpre_a, dpre_b)


def run_down_grad(dout_a, dout_b, act_a, act_b):
    slots, width = dout_a.shape
    inner = act_a.shape[1]
    tile = inner // 6
    whole = pl.BlockSpec((slots, width), lambda j: (0, 0))
    part = pl.BlockSpec((slots, tile), lambda j: (0, j))
    return pl.pallas_call(
        down_grad_kernel,
        grid=(6,),
        out_shape=shape((inner, width), f32),
        in_specs=[whole, whole, part, part],
        out_specs=pl.BlockSpec((tile, width), lambda j: (j, 0)),
        compiler_params=params(),
        cost_estimate=cost(10),
        name="down_gradient",
    )(dout_a, dout_b, act_a, act_b)


def swap(block):
    return lax.ppermute(block, "section", [(0, 1), (1, 0)])


def across(block, bit, devices):
    return lax.ppermute(block, "expert", [(i, i ^ (1 << bit)) for i in range(devices)])


def bit_orders(bits):
    if bits == 4:
        return [(3, 2, 0, 1), (3, 0, 1, 2), (3, 1, 2, 0)]
    names = list(range(bits))
    return [tuple(names[(i + r * bits // pieces) % bits] for i in names) for r in range(pieces)]


def split_lanes(block):
    step = block.shape[-1] // pieces
    return [block[..., p * step : (p + 1) * step] for p in range(pieces)]


def token_of(block):
    value = block[(0,) * block.ndim]
    return (value != value).astype(jnp.int32)


def gathered(shards, device, devices, after):
    bits = devices.bit_length() - 1
    orders = bit_orders(bits)
    rows = shards[0].shape[1]
    if rows % 16:
        found = [p.reshape(p.shape[:1] + (1,) * bits + p.shape[1:]) for p in shards]
        for step in range(bits):
            for p in range(pieces):
                bit = orders[p][step]
                axis = bits - bit
                got = across(found[p], bit, devices)
                high = (device >> bit) & 1 == 1
                found[p] = jnp.where(
                    high,
                    jnp.concatenate([got, found[p]], axis),
                    jnp.concatenate([found[p], got], axis),
                )
        found = [p.reshape(1, p.shape[0], -1, p.shape[-1]) for p in found]
        return [[[0]]] * pieces, False, [*found, *[swap(p) for p in found]]
    me = device.astype(jnp.int32).reshape(1)
    found = [p[None] for p in shards]
    differ = [[0] for _ in shards]
    for step in range(bits - 1):
        gots = [across(found[p], orders[p][step], devices) for p in range(pieces)]
        outs = [shape((2 * p.shape[0],) + p.shape[1:]) for p in found]
        last = after if step == bits - 2 else ()
        found = run(join_kernel, "join", 3, [*found, *gots], outs, [], me, (), last)[1:]
        for p in range(pieces):
            differ[p] = differ[p] + [d ^ (1 << orders[p][step]) for d in differ[p]]
    far = [across(found[p], orders[p][-1], devices) for p in range(pieces)]
    layout = [
        [differ[p], [d ^ (1 << orders[p][-1]) for d in differ[p]]] for p in range(pieces)
    ]
    near_other = [swap(p) for p in found]
    far_other = [swap(p) for p in far]
    arrays = []
    for near, distant in ((found, far), (near_other, far_other)):
        for p in range(pieces):
            arrays += [near[p], distant[p]]
    return layout, True, arrays


def halved(block, bit, bits, lead, device, devices, late=0):
    axis = lead + bits - 1 - bit
    low = lax.index_in_dim(block, 0, axis, keepdims=True)
    high = lax.index_in_dim(block, 1, axis, keepdims=True)
    got = across(jnp.where((device >> bit) & 1 == 1, low, high), bit, devices)
    up = ((device + late) >> bit) & 1 == 1
    return jnp.where(up, high, low).astype(f32) + got.astype(f32)


def folded(found, step, device, devices, late=0):
    bits = devices.bit_length() - 1
    orders = [order[::-1] for order in bit_orders(bits)]
    results = []
    for p in range(pieces):
        value = halved(found[p], orders[p][step], bits, 1, device, devices, late)
        results.append(value if step == bits - 1 else value.astype(bf16))
    return results


def unfolded(total, devices):
    bits = devices.bit_length() - 1
    return [
        p.reshape(p.shape[:1] + (2,) * bits + (p.shape[1] // devices, p.shape[2]))
        for p in split_lanes(total)
    ]


def body(
    block_input,
    cotangent,
    lengths,
    routes,
    norm_gain,
    attention_in,
    attention_out,
    position_bias,
    router,
    expert_up,
    expert_down,
):
    _, rows, width = block_input.shape
    section = lax.axis_index("section")
    device = lax.axis_index("expert")
    devices = lax.axis_size("expert")
    bits = devices.bit_length() - 1
    first = section == 0
    mine = [(section == which).astype(jnp.int32).reshape(1) for which in range(2)]
    experts = router.shape[2]
    shard_rows = router.shape[1]
    buckets, heads = position_bias.shape[1:]
    capacity = max(2, 3 * rows // (2 * experts))
    capacity = -(-capacity // 8) * 8
    slots = experts * capacity

    def both(own, other):
        return (jnp.where(first, own, other), jnp.where(first, other, own))

    def own_micro(block):
        return jnp.where(first, block[0], block[1])

    def other_micro(block):
        return jnp.where(first, block[1], block[0])

    own_shards = jnp.concatenate([attention_in[0], attention_out], axis=0)
    cut = split_lanes(own_shards)
    pad = cut[0].shape[-1] - experts
    cut[0] = jnp.concatenate([cut[0], jnp.pad(router, ((0, 0), (0, 0), (0, pad)))], axis=0)
    small_parts = (
        norm_gain[0].reshape(-1),
        position_bias[0].reshape(-1),
        other_micro(routes[0])[:, 0].astype(f32),
    )
    small = jnp.concatenate(small_parts)
    small = jnp.pad(small, (0, -small.shape[0] % 128)).reshape(-1, 128)
    small_given = swap(small).reshape(-1)
    split_at, at = [], 0
    for part in small_parts:
        at += part.shape[0]
        split_at.append(at)
    gain_other, table_other, route_other, _ = jnp.split(small_given, split_at)
    gains = both(norm_gain[0], gain_other.reshape(2, width))
    tables = both(position_bias[0], table_other.reshape(buckets, heads))
    route_pair = both(own_micro(routes[0])[:, 0], route_other.astype(jnp.int32))

    positions = jnp.arange(rows, dtype=jnp.int32)
    bounds = jnp.cumsum(own_micro(lengths)[0])
    segment = jnp.sum((positions[:, None] >= bounds[None, :]).astype(jnp.int32), axis=1)
    seg_col, seg_row = segment[:, None], segment[None, :]
    offsets = jnp.arange(2 * rows, dtype=jnp.int32) - (rows - 1)
    bucket_hot = (
        bucket_of(offsets)[:, None] == jnp.arange(buckets, dtype=jnp.int32)[None, :]
    ).astype(f32)
    lines = [
        lax.dot_general(table, bucket_hot, (((0,), (1,)), ((), ())), precision=highest)
        for table in tables
    ]
    bases = [run_bias(line, rows) for line in lines]
    before = (positions[:, None] > positions[None, :]).astype(bf16)
    places = []
    for route in route_pair:
        chosen = route[:, None] == jnp.arange(experts, dtype=jnp.int32)[None, :]
        earlier = dot(before, chosen.astype(bf16))
        slot = jnp.sum(jnp.where(chosen, earlier, 0.0), axis=1).astype(jnp.int32)
        places.append(route * capacity + slot)
    route_cols = [route[:, None] for route in route_pair]
    place_cols = [place[:, None] for place in places]
    place_rows = [place[None, :] for place in places]
    layout, apart, weights = gathered(
        cut, device, devices, (*bases, *place_rows, *place_cols, *route_cols, seg_col, seg_row, *gains)
    )
    core = jnp.stack([section, device if apart else jnp.zeros_like(device)]).astype(jnp.int32)
    up_other = swap(expert_up[0, 0])
    down_other = swap(expert_down[0, 0])
    ups, downs = (expert_up[0, 0], up_other), (expert_down[0, 0], down_other)

    def exchanged(block):
        return lax.all_to_all(block, "expert", split_axis=0, concat_axis=0, tiled=True)

    def expert_forward(which, arrived):
        return run_expert(
            expert_forward_kernel, mine[which], arrived, (), ups, downs, 2, 11, "expert_forward"
        )

    def expert_backward(mine, arrived, slope):
        return run_expert(
            expert_backward_kernel, mine, arrived, (slope,), ups, downs, 1, 11,
            "expert_backward",
        )

    def shared_inputs(which):
        return (
            gains[which], bases[which], seg_col, seg_row, route_cols[which],
        )

    inputs = own_micro(block_input)
    cot = own_micro(cotangent)
    token, q0, k0, v0, o0, p0, mid0, h20, share0, gate0, send0 = run_forward(
        False, layout, core, weights, (inputs, *shared_inputs(0), place_rows[0]), slots, experts,
        heads, (),
    )
    buf0 = exchanged(send0)
    act0, slope0, result0 = expert_forward(0, buf0)
    back0 = exchanged(result0)
    _, q1, k1, v1, o1, p1, mid1, h21, share1, gate1, send1, between, combined0, grad_send1 = (
        run_forward(
            True, layout, core, weights,
            (mid0, gate0, place_cols[0], back0, cot, *shared_inputs(1), place_rows[1]),
            slots, experts, heads, (),
        )
    )
    buf1 = exchanged(send1)
    dout1 = exchanged(grad_send1)
    act1, slope1, result1 = expert_forward(1, buf1)
    dpre1, dbuf1 = expert_backward(mine[1], dout1, slope1)
    back1 = exchanged(
        jnp.concatenate(
            [block.reshape(experts, capacity, width) for block in (result1, dbuf1)], axis=1
        ).reshape(2 * slots, width)
    )
    place_out = place_cols[1] + route_cols[1] * capacity
    _, dx11, low1, dq1, dk1, dv1, router_grad1, gain_two1, line_grad1, last = run_heads_backward(
        True, layout, core, weights,
        (q1, k1, v1, p1, mid1, h21, share1, gate1, cot, back1, place_out, gains[1],
         route_cols[1], place_out + capacity),
        experts, (),
    )
    token, dx1, gain_one1, dy0, grad_send0 = run_input_backward(
        True, layout, core, weights,
        (between, dx11, dq1, dk1, dv1, gains[1], gate0, place_rows[0]), slots, (),
    )
    token, keep1, give1 = run_weight_backward(
        core + token[0], (between, gains[1], o1, low1, dq1, dk1, dv1), ()
    )
    dout0 = exchanged(grad_send0)

    given1 = swap(give1)
    dpre0, dbuf0 = expert_backward(mine[0] + token[0], dout0, slope0)
    dback0 = exchanged(dbuf0)
    from_first = [swap(block) for block in (buf1, act1, dout1, dpre1)]
    from_second = [swap(block) for block in (buf0, act0, dout0, dpre0)]

    def up_of(bufs, dpres):
        return run_up_grad(*bufs, *dpres)

    def down_of(douts, acts):
        return run_down_grad(*douts, *acts)

    up_sets = ((buf0, from_second[0], dpre0, from_second[3]), (buf1, from_first[0], dpre1, from_first[3]))
    down_sets = ((dout0, from_second[2], act0, from_second[1]), (dout1, from_first[2], act1, from_first[1]))

    def own_layer(run_grad, sets, token):
        return lax.cond(
            section + token == 0, lambda a, b: run_grad(*a), lambda a, b: run_grad(*b), *sets
        )

    grads = [
        functools.partial(own_layer, run_down_grad, down_sets),
        functools.partial(own_layer, run_up_grad, up_sets),
    ]

    grad_down = grads[0](token_of(dbuf0))
    token, dx10, low0, dq0, dk0, dv0, router_grad0, gain_two0, line_grad0 = run_heads_backward(
        False, layout, core, weights,
        (q0, k0, v0, p0, mid0, h20, share0, gate0, dy0, dback0, combined0, gains[0],
         route_cols[0], place_cols[0]),
        experts, (grad_down,),
    )
    token, keep0, give0 = run_weight_backward(
        core, (inputs, gains[0], o0, low0, dq0, dk0, dv0), ()
    )
    _, dx0, gain_one0 = run_input_backward(
        False, layout, core + token[0], weights, (inputs, dx10, dq0, dk0, dv0, gains[0]), slots, ()
    )

    little = [
        jnp.concatenate(parts, axis=0)
        for parts in (
            (gain_one0, gain_two0, line_grad0, router_grad0),
            (gain_one1, gain_two1, line_grad1, router_grad1),
        )
    ]
    little = jnp.where(first, little[0], little[1]) + swap(jnp.where(first, little[1], little[0]))
    sums, little_sum, (grad_up,) = summed_blocks(
        [keep0, swap(give0), keep1, given1], little, device, devices, grads[1:], (dx0,)
    )
    shared0, shared1 = sums[:2], sums[2:]
    shared_other = swap(jnp.where(first, shared1, shared0))
    queries_keys = jnp.where(first, shared0, shared_other)
    values_out = jnp.where(first, shared_other, shared1)

    grad_table = jnp.dot(little_sum[2 : 2 + heads], bucket_hot, precision=highest).T
    router_sum = lax.dynamic_slice_in_dim(little_sum[2 + heads :], device * shard_rows, shard_rows, 1)

    out_other = swap(jnp.where(first, last, between))
    layer_out = jnp.stack(
        [jnp.where(first, between, out_other), jnp.where(first, out_other, last)]
    )
    grad_other = swap(jnp.where(first, dx1, dx0))
    input_grad = jnp.stack([jnp.where(first, dx0, grad_other), jnp.where(first, grad_other, dx1)])
    return (
        layer_out[None],
        input_grad[None],
        little_sum[:2][None],
        jnp.concatenate([queries_keys, values_out[:1]], axis=0)[None],
        values_out[1][None],
        grad_table[None],
        router_sum.T[None],
        grad_up[None, None],
        grad_down[None, None],
    )


def solution(mesh):
    in_specs = (
        P(None, "expert", None),
        P(None, "expert", None),
        P(None, "expert", None),
        P("section", None, "expert", None),
        P("section", None, None),
        P("section", None, "expert", None),
        P("section", "expert", None),
        P("section", None, None),
        P("section", "expert", None),
        P("section", "expert", None, None),
        P("section", "expert", None, None),
    )
    out_specs = (
        P("section", None, "expert", None),
        P("section", None, "expert", None),
        P("section", None, None),
        P("section", None, "expert", None),
        P("section", "expert", None),
        P("section", None, None),
        P("section", "expert", None),
        P("section", "expert", None, None),
        P("section", "expert", None, None),
    )
    return jax.shard_map(body, mesh=mesh, in_specs=in_specs, out_specs=out_specs, check_vma=False)
```

```python
import functools

import jax
import jax.numpy as jnp
from jax import lax
from jax.experimental import pallas as pl
from jax.experimental.pallas import tpu as pltpu
from jax.sharding import PartitionSpec as P

bucket_edges = (12, 16, 23, 32, 46, 64, 91)
norm_eps = 1e-06
gelu_c = 0.7978845608028654
gelu_cube = 0.044715
masked_score = -1e30
highest = lax.Precision.HIGHEST
f32 = jnp.float32
bf16 = jnp.bfloat16
vmem_bytes = 56 * 2**20
pieces = 3


def dot(left, right):
    return jnp.dot(left, right, preferred_element_type=f32)


def dot_lead(left, right):
    return lax.dot_general(left, right, (((0,), (0,)), ((), ())), preferred_element_type=f32)


def dot_last(left, right):
    return lax.dot_general(left, right, (((1,), (1,)), ((), ())), preferred_element_type=f32)


def gelu_pair(value):
    square = value * value
    inner = jnp.tanh(gelu_c * value * (1.0 + gelu_cube * square))
    half = 0.5 * (1.0 + inner)
    slope = half + 0.5 * value * (1.0 - inner * inner) * (
        gelu_c * (1.0 + 3.0 * gelu_cube * square)
    )
    return (value * half, slope)


def bucket_of(offset):
    distance = jnp.abs(offset)
    found = 16 * (offset > 0).astype(jnp.int32) + jnp.minimum(distance, 8)
    for edge in bucket_edges:
        found = found + (distance >= edge).astype(jnp.int32)
    return found


def norm_scale(values):
    return lax.rsqrt(jnp.mean(values * values, axis=-1, keepdims=True) + norm_eps)


def norm_backward(values, gain, grad_normed):
    scale = norm_scale(values)
    normal = values * scale
    inner = grad_normed * gain
    grad_values = scale * (inner - normal * jnp.mean(inner * normal, axis=-1, keepdims=True))
    return (grad_values, jnp.sum(grad_normed * normal, axis=0, keepdims=True))


def zero_token(token_ref):
    token_ref[0] = 0


def weight_copies(place_ref, layer, matrices, blocks, weights, router, sems):
    core, device = place_ref[0], place_ref[1]
    first, count = matrices
    copies = []
    for p in range(pieces):
        for (here, differ), (there, _) in zip(blocks[0][p], blocks[1][p]):
            rows, step = here.shape[2:]
            for at in range(here.shape[0]):
                target = pl.ds(pl.multiple_of((device ^ differ[at]) * rows, rows), rows)
                couples = [
                    (pl.ds(first, count), pl.ds(0, step), weights.at[:, target, pl.ds(p * step, step)])
                ]
                if p == 0 and router is not None:
                    couples.append((4, pl.ds(0, 128), router.at[target, :]))
                for which, lanes, goal in couples:
                    sem = sems.at[len(copies)]
                    own = pltpu.make_async_copy(here.at[at, which, :, lanes], goal, sem)
                    other = pltpu.make_async_copy(there.at[at, which, :, lanes], goal, sem)
                    copies.append(own)
                    pl.when(core == layer)(own.start)
                    pl.when(core != layer)(other.start)
    return copies


def laid_out(layout, refs):
    blocks, at = [], 0
    for _ in range(2):
        blocks.append([])
        for piece in layout:
            blocks[-1].append([(refs[at + i], differ) for i, differ in enumerate(piece)])
            at += len(piece)
    return blocks, refs[at:]


def join_kernel(place_ref, *refs):
    olds, gots, outs = refs[:pieces], refs[pieces : 2 * pieces], refs[2 * pieces :]
    token_ref, outs = outs[0], outs[1:]
    zero_token(token_ref)
    for old, got, out in zip(olds, gots, outs):
        half = old.shape[0]
        out[:half] = old[...]
        out[half:] = got[...]


def head_masks():
    lane = lax.broadcasted_iota(jnp.int32, (1, 128), 1)
    low = (lane < 64).astype(f32)
    return (low.astype(bf16), (1.0 - low).astype(bf16))


def bias_kernel(line_ref, base_ref):
    heads, _, reach = base_ref.shape
    wide = line_ref.shape[1]

    def one(head, carry):
        line = jnp.broadcast_to(line_ref[pl.ds(head, 1), :], (128, wide))
        turned = pltpu.roll(line, wide - 127, 1, stride=1, stride_axis=0)
        base_ref[head] = turned[:, :reach]
        return carry

    lax.fori_loop(0, heads, one, 0)


def bias_of(base_ref, head, rows):
    blocks = rows // 128
    return jnp.concatenate(
        [base_ref[head, :, 128 * (blocks - 1 - a) : 128 * (blocks - 1 - a) + rows] for a in range(blocks)],
        axis=0,
    )


def diagonal_line(grad_scores, flip, wide):
    blocks = grad_scores.shape[0] // 128
    parts = [None] * (wide // 128)
    for a in range(blocks):
        flipped = dot(flip, grad_scores[128 * a : 128 * (a + 1), :])
        for j in range(blocks):
            piece = flipped[:, 128 * j : 128 * (j + 1)]
            at = j + blocks - 1 - a
            parts[at] = piece if parts[at] is None else parts[at] + piece
    empty = jnp.zeros((128, 128), f32)
    sums = jnp.concatenate([empty if part is None else part for part in parts], axis=1)
    turned = pltpu.roll(sums, 0, 1, stride=1, stride_axis=0)
    return jnp.sum(turned, axis=0, keepdims=True)


def one_hot_columns(place_col, slots):
    rows = place_col.shape[0]
    return (place_col == lax.broadcasted_iota(jnp.int32, (rows, slots), 1)).astype(f32).astype(bf16)


def one_hot_rows(place_row, slots):
    rows = place_row.shape[1]
    return (place_row == lax.broadcasted_iota(jnp.int32, (slots, rows), 0)).astype(f32).astype(bf16)


def forward_kernel(second, experts, layout, core_ref, *refs):
    blocks, refs = laid_out(layout, refs)
    base_hbm, refs = refs[0], refs[1:]
    if second:
        (before_ref, gate_before_ref, place_before_ref, back_ref, cot_ref), refs = refs[:5], refs[5:]
    else:
        (x_ref,), refs = refs[:1], refs[1:]
    (gain_ref, seg_col_ref, seg_row_ref, route_ref, place_ref), refs = refs[:5], refs[5:]
    (
        token_ref, q_ref, k_ref, v_ref, o_ref, p_hbm, mid_ref, h2_ref, share_ref, gate_ref, send_ref,
    ), refs = refs[:11], refs[11:]
    if second:
        (x_out_ref, combined_ref, grad_send_ref), refs = refs[:3], refs[3:]
    weights, router_ref, mask_ref, base_ref, p_ref, part_sems, sems = refs
    zero_token(token_ref)
    copies = weight_copies(core_ref, int(second), (0, 4), blocks, weights, router_ref, sems)
    base_copy = pltpu.make_async_copy(base_hbm, base_ref, part_sems.at[0])
    base_copy.start()
    slots = send_ref.shape[0]
    rows = q_ref.shape[0]
    if second:
        scatter = one_hot_columns(place_before_ref[...], slots)
        combined = dot(scatter, back_ref[...])
        combined_ref[...] = combined.astype(bf16)
        low = (before_ref[...] + gate_before_ref[...] * combined).astype(bf16)
        x_out_ref[...] = low
        wide = low.astype(f32)
    else:
        wide = x_ref[...].astype(f32)
    h1 = (wide * norm_scale(wide) * gain_ref[0:1, :]).astype(bf16)
    mask_ref[...] = jnp.where(seg_col_ref[...] == seg_row_ref[...], 0.0, masked_score)
    for copy in copies:
        copy.wait()
    q_ref[...] = dot(h1, weights[0]).astype(bf16)
    k_ref[...] = dot(h1, weights[1]).astype(bf16)
    v_ref[...] = dot(h1, weights[2]).astype(bf16)
    masks = head_masks()
    base_copy.wait()

    def leaving(p):
        both = pl.ds(2 * p, 2)
        return pltpu.make_async_copy(p_ref.at[both], p_hbm.at[both], part_sems.at[1 + p])

    def pair(p, carry):
        columns = pl.ds(pl.multiple_of(p * 128, 128), 128)
        queries, keys, values = q_ref[:, columns], k_ref[:, columns], v_ref[:, columns]
        mixed = jnp.zeros((rows, 128), f32)
        for half in range(2):
            head = 2 * p + half
            scores = dot_last(queries * masks[half], keys) * 0.125 + bias_of(base_ref, head, rows)
            scores = scores + mask_ref[...]
            raised = jnp.exp(scores - jnp.max(scores, axis=-1, keepdims=True))
            total = jnp.sum(raised, axis=-1, keepdims=True)
            shares = (raised * (1.0 / total)).astype(bf16)
            p_ref[head] = shares
            mixed = mixed + dot(shares, values * masks[half])
        o_ref[:, columns] = mixed.astype(bf16)
        leaving(p).start()
        return carry

    lax.fori_loop(0, p_ref.shape[0] // 2, pair, 0)
    middle = wide + dot(o_ref[...], weights[3])
    mid_ref[...] = middle
    h2 = (middle * norm_scale(middle) * gain_ref[1:2, :]).astype(bf16)
    h2_ref[...] = h2
    logits = dot(h2, router_ref[...])
    lane = lax.broadcasted_iota(jnp.int32, (1, 128), 1)
    logits = jnp.where(lane < experts, logits, masked_score)
    raised = jnp.exp(logits - jnp.max(logits, axis=-1, keepdims=True))
    shares = raised / jnp.sum(raised, axis=-1, keepdims=True)
    share_ref[...] = shares
    chosen = route_ref[...] == lax.broadcasted_iota(jnp.int32, shares.shape, 1)
    gate = jnp.sum(jnp.where(chosen, shares, 0.0), axis=-1, keepdims=True)
    gate_ref[...] = gate
    gather = one_hot_rows(place_ref[...], slots)
    send_ref[...] = dot(gather, h2).astype(bf16)
    if second:
        grad_out = (gate * cot_ref[...].astype(f32)).astype(bf16)
        grad_send_ref[...] = dot(gather, grad_out).astype(bf16)
    for p in range(p_ref.shape[0] // 2):
        leaving(p).wait()


def heads_backward_kernel(second, layout, core_ref, *refs):
    blocks, refs = laid_out(layout, refs)
    p_hbm, refs = refs[0], refs[1:]
    (
        q_ref, k_ref, v_ref, mid_ref, h2_ref, share_ref, gate_ref, dy_ref, dback_ref,
        out_ref, gain_ref, route_ref, place_ref,
    ), refs = refs[:13], refs[13:]
    (
        token_ref, dx1_ref, low_ref, dq_ref, dk_ref, dv_ref, router_grad_ref, gain_grad_ref,
        line_grad_ref,
    ), refs = refs[:9], refs[9:]
    if second:
        (y_ref,), refs = refs[:1], refs[1:]
    weights, router_ref, do_ref, p_ref, part_sems, sems = refs
    zero_token(token_ref)

    def arriving(p):
        both = pl.ds(2 * p, 2)
        return pltpu.make_async_copy(p_hbm.at[both], p_ref.at[both], part_sems.at[p])

    copies = weight_copies(core_ref, int(second), (3, 1), blocks, weights, router_ref, sems)
    for p in range(p_ref.shape[0] // 2):
        arriving(p).start()
    rows = q_ref.shape[0]
    slots = dback_ref.shape[0]
    dy = dy_ref[...].astype(f32)
    gate = gate_ref[...]
    middle = mid_ref[...]
    scatter = one_hot_columns(place_ref[...], slots)
    if second:
        combined = dot(one_hot_columns(out_ref[...], slots), dback_ref[...])
        y_ref[...] = (middle + gate * combined).astype(bf16)
    else:
        combined = out_ref[...].astype(f32)
    grad_gate = jnp.sum(dy * combined, axis=-1, keepdims=True)
    shares = share_ref[...]
    chosen = route_ref[...] == lax.broadcasted_iota(jnp.int32, shares.shape, 1)
    grad_logits = (grad_gate * gate * (chosen.astype(f32) - shares)).astype(bf16)
    router_grad_ref[...] = dot_lead(grad_logits, h2_ref[...])[: router_grad_ref.shape[0]]
    for copy in copies:
        copy.wait()
    grad_two = dot(scatter, dback_ref[...]) + dot_last(grad_logits, router_ref[...])
    grad_middle, gain_two = norm_backward(middle, gain_ref[1:2, :], grad_two)
    gain_grad_ref[...] = gain_two
    grad_middle = grad_middle + dy
    dx1_ref[...] = grad_middle
    low = grad_middle.astype(bf16)
    low_ref[...] = low
    do_ref[...] = dot_last(low, weights[0]).astype(bf16)
    masks = head_masks()
    flip = (
        lax.broadcasted_iota(jnp.int32, (128, 128), 0)
        + lax.broadcasted_iota(jnp.int32, (128, 128), 1)
        == 127
    )
    flip = flip.astype(f32).astype(bf16)

    def pair(p, carry):
        arriving(p).wait()
        columns = pl.ds(pl.multiple_of(p * 128, 128), 128)
        queries, keys, values = q_ref[:, columns], k_ref[:, columns], v_ref[:, columns]
        grad_mixed = do_ref[:, columns]
        dq = jnp.zeros((rows, 128), f32)
        dk = jnp.zeros((rows, 128), f32)
        dv = jnp.zeros((rows, 128), f32)
        for half in range(2):
            head = 2 * p + half
            own_mixed = grad_mixed * masks[half]
            low_shares = p_ref[head]
            shares = low_shares.astype(f32)
            grad_shares = dot_last(own_mixed, values)
            mean = jnp.sum(shares * grad_shares, axis=-1, keepdims=True)
            grad_scores = (shares * (grad_shares - mean)).astype(bf16)
            dv = dv + dot_lead(low_shares, own_mixed)
            dq = dq + dot(grad_scores, keys * masks[half])
            dk = dk + dot_lead(grad_scores, queries * masks[half])
            line_grad_ref[pl.ds(head, 1), :] = diagonal_line(
                grad_scores, flip, line_grad_ref.shape[1]
            )
        dq_ref[:, columns] = (dq * 0.125).astype(bf16)
        dk_ref[:, columns] = (dk * 0.125).astype(bf16)
        dv_ref[:, columns] = dv.astype(bf16)
        return carry

    lax.fori_loop(0, p_ref.shape[0] // 2, pair, 0)


def input_backward_kernel(second, layout, core_ref, *refs):
    blocks, refs = laid_out(layout, refs)
    (x_ref, dx1_ref, dq_ref, dk_ref, dv_ref, gain_ref), refs = refs[:6], refs[6:]
    if second:
        (gate_next_ref, place_next_ref), refs = refs[:2], refs[2:]
    (token_ref, dx_ref, gain_grad_ref), refs = refs[:3], refs[3:]
    if second:
        (low_out_ref, grad_send_ref), refs = refs[:2], refs[2:]
    weights, sems = refs
    zero_token(token_ref)
    copies = weight_copies(core_ref, int(second), (0, 3), blocks, weights, None, sems)
    for copy in copies:
        copy.wait()
    wide = x_ref[...].astype(f32)
    grad_one = (
        dot_last(dq_ref[...], weights[0])
        + dot_last(dk_ref[...], weights[1])
        + dot_last(dv_ref[...], weights[2])
    )
    grad_inputs, gain_one = norm_backward(wide, gain_ref[0:1, :], grad_one)
    grad_inputs = grad_inputs + dx1_ref[...]
    dx_ref[...] = grad_inputs
    gain_grad_ref[...] = gain_one
    if second:
        low = grad_inputs.astype(bf16)
        low_out_ref[...] = low
        grad_out = (gate_next_ref[...] * low.astype(f32)).astype(bf16)
        gather = one_hot_rows(place_next_ref[...], grad_send_ref.shape[0])
        grad_send_ref[...] = dot(gather, grad_out).astype(bf16)


def weight_backward_kernel(core_ref, x_ref, gain_ref, o_ref, low_ref, dq_ref, dk_ref, dv_ref, *refs):
    token_ref, keep_ref, give_ref = refs
    zero_token(token_ref)
    core = core_ref[0]

    def put(matrix, value):
        value = value.astype(bf16)

        @pl.when(core == matrix // 2)
        def _():
            keep_ref[matrix % 2] = value

        @pl.when(core != matrix // 2)
        def _():
            give_ref[matrix % 2] = value

    wide = x_ref[...].astype(f32)
    h1 = (wide * norm_scale(wide) * gain_ref[0:1, :]).astype(bf16)
    put(0, dot_lead(h1, dq_ref[...]))
    put(1, dot_lead(h1, dk_ref[...]))
    put(2, dot_lead(h1, dv_ref[...]))
    put(3, dot_lead(o_ref[...], low_ref[...]))


def places_of(block, order):
    place = 0
    for bit in order:
        place = 2 * place + ((block >> bit) & 1)
    return place


def fold_first_kernel(orders, device_ref, *refs):
    sums, outs = refs[:4], refs[4:]
    token_ref, outs = outs[0], outs[1:]
    zero_token(token_ref)
    keeps, sends = outs[:pieces], outs[pieces:]
    device = device_ref[0]
    half, rows, step = keeps[0].shape[1:]
    for block in range(2 * half):
        at = pl.ds(pl.multiple_of((device ^ block) * rows, rows), rows)
        for layer in range(2):
            for matrix in range(2):
                total = sums[2 * layer][matrix, at, :].astype(f32)
                total = (total + sums[2 * layer + 1][matrix, at, :].astype(f32)).astype(bf16)
                for p in range(pieces):
                    place = places_of(block, orders[p])
                    target = sends[p] if place >= half else keeps[p]
                    target[2 * layer + matrix, place % half] = total[:, p * step : (p + 1) * step]


def fold_kernel(device_ref, *refs):
    olds, gots, outs = refs[:pieces], refs[pieces : 2 * pieces], refs[2 * pieces :]
    token_ref, outs = outs[0], outs[1:]
    zero_token(token_ref)
    for p in range(pieces):
        total = olds[p][...].astype(f32) + gots[p][...].astype(f32)
        half = total.shape[1] // 2
        outs[p][...] = total[:, :half].astype(bf16)
        outs[pieces + p][...] = total[:, half:].astype(bf16)


def fold_last_kernel(device_ref, *refs):
    olds, gots, (token_ref, out_ref) = refs[:pieces], refs[pieces : 2 * pieces], refs[2 * pieces :]
    zero_token(token_ref)
    for p in range(pieces):
        step = olds[p].shape[3]
        total = olds[p][...].astype(f32) + gots[p][...].astype(f32)
        out_ref[:, :, p * step : (p + 1) * step] = total[:, 0]


def expert_copies(mine, tiles, up_refs, down_refs, up, down, sems, start):
    width = up.shape[2]

    def copies(which):
        found = []
        for j in range(tiles):
            at = pl.ds(j * width, width)
            found.append(
                (
                    pltpu.make_async_copy(up_refs[which].at[:, at], up.at[j], sems.at[0, j]),
                    pltpu.make_async_copy(down_refs[which].at[at, :], down.at[j], sems.at[1, j]),
                )
            )
        return found

    if start:
        for which in range(2):

            @pl.when(mine == 1 - which)
            def _():
                for couple in copies(which):
                    for copy in couple:
                        copy.start()


def expert_wait(j, up_ref, down_ref, up, down, sems):
    width = up.shape[2]
    at = pl.ds(0, width)
    pltpu.make_async_copy(up_ref.at[:, at], up.at[j], sems.at[0, j]).wait()
    pltpu.make_async_copy(down_ref.at[at, :], down.at[j], sems.at[1, j]).wait()


def expert_forward_kernel(
    mine_ref, x_ref, up_own, up_other, down_own, down_other, act_ref, slope_ref, out_ref,
    up, down, total, sems,
):
    j = pl.program_id(0)
    tiles = up.shape[0]

    @pl.when(j == 0)
    def _():
        expert_copies(
            mine_ref[0], tiles, (up_own, up_other), (down_own, down_other), up, down, sems, True
        )
        total[...] = jnp.zeros_like(total)

    expert_wait(j, up_own, down_own, up, down, sems)
    active, slope = gelu_pair(dot(x_ref[...], up[j]))
    active = active.astype(bf16)
    act_ref[...] = active
    slope_ref[...] = slope.astype(bf16)
    total[...] += dot(active, down[j])

    @pl.when(j == tiles - 1)
    def _():
        out_ref[...] = total[...].astype(bf16)


def expert_backward_kernel(
    mine_ref, dout_ref, slope_ref, up_own, up_other, down_own, down_other, dpre_ref, dbuf_ref,
    up, down, total, sems,
):
    j = pl.program_id(0)
    tiles = up.shape[0]

    @pl.when(j == 0)
    def _():
        expert_copies(
            mine_ref[0], tiles, (up_own, up_other), (down_own, down_other), up, down, sems, True
        )
        total[...] = jnp.zeros_like(total)

    expert_wait(j, up_own, down_own, up, down, sems)
    grad_pre = (dot_last(dout_ref[...], down[j]) * slope_ref[...].astype(f32)).astype(bf16)
    dpre_ref[...] = grad_pre
    total[...] += dot_last(grad_pre, up[j])

    @pl.when(j == tiles - 1)
    def _():
        dbuf_ref[...] = total[...].astype(bf16)


def up_grad_kernel(buf_a, buf_b, dpre_a, dpre_b, grad_ref):
    grad_ref[...] = dot_lead(buf_a[...], dpre_a[...]) + dot_lead(buf_b[...], dpre_b[...])


def down_grad_kernel(dout_a, dout_b, act_a, act_b, grad_ref):
    grad_ref[...] = dot_lead(act_a[...], dout_a[...]) + dot_lead(act_b[...], dout_b[...])


def shape(dims, kind=bf16):
    return jax.ShapeDtypeStruct(dims, kind)


def params():
    return pltpu.CompilerParams(vmem_limit_bytes=vmem_bytes)


def cost(us):
    return pl.CostEstimate(flops=int(us * 1e9), bytes_accessed=0, transcendentals=0)


smem = pl.BlockSpec(memory_space=pltpu.SMEM)
vmem = pl.BlockSpec(memory_space=pltpu.VMEM)
anywhere = pl.BlockSpec(memory_space=pl.ANY)
hbm = pl.BlockSpec(memory_space=pltpu.HBM)


def run(kernel, name, us, inputs, outs, scratch, core, weights=(), after=(), apart=()):
    def marked(core_ref, *refs):
        at = len(weights) + len(inputs)
        return kernel(core_ref, *refs[:at], *refs[at + len(after) :])

    outs = [shape((1,), jnp.int32)] + list(outs)
    return pl.pallas_call(
        marked,
        out_shape=outs,
        in_specs=[smem]
        + [anywhere] * len(weights)
        + [vmem] * len(inputs)
        + [anywhere] * len(after),
        out_specs=[smem] + [hbm if at in apart else vmem for at in range(len(outs) - 1)],
        scratch_shapes=scratch,
        compiler_params=params(),
        cost_estimate=cost(us),
        name=name,
    )(core, *weights, *inputs, *after)


def weight_scratch(layout, count, width, router):
    copies = sum(len(differ) for piece in layout for differ in piece)
    held = [pltpu.VMEM((count, width, width), bf16)]
    if router:
        copies += sum(len(differ) for differ in layout[0])
        held.append(pltpu.VMEM((width, 128), bf16))
    return held, [pltpu.SemaphoreType.DMA((copies,))]


def run_bias(line, rows):
    heads, wide = line.shape
    return pl.pallas_call(
        bias_kernel,
        out_shape=shape((heads, 128, 2 * rows - 128), f32),
        in_specs=[vmem],
        out_specs=vmem,
        compiler_params=params(),
        cost_estimate=cost(3),
        name="bias_base",
    )(line)


def run_forward(second, layout, core, weights, inputs, slots, experts, heads, after):
    rows, width = inputs[0].shape
    outs = [shape((rows, width))] * 4 + [
        shape((heads, rows, rows)),
        shape((rows, width), f32),
        shape((rows, width)),
        shape((rows, 128), f32),
        shape((rows, 1), f32),
        shape((slots, width)),
    ]
    if second:
        outs += [shape((rows, width)), shape((rows, width)), shape((slots, width))]
    held, sems = weight_scratch(layout, 4, width, True)
    return run(
        functools.partial(forward_kernel, second, experts, layout), "attention_forward", 15, inputs, outs,
        held + [pltpu.VMEM((rows, rows), f32)]
        + [pltpu.VMEM((heads, 128, 2 * rows - 128), f32), pltpu.VMEM((heads, rows, rows), bf16)]
        + [pltpu.SemaphoreType.DMA((1 + heads // 2,))] + sems, core, weights, after, (4,),
    )


def run_heads_backward(second, layout, core, weights, inputs, experts, after):
    rows, width = inputs[0].shape
    heads = weights[-1].shape[0]
    outs = [shape((rows, width), f32)] + [shape((rows, width))] * 4 + [
        shape((experts, width), f32),
        shape((1, width), f32),
        shape((heads, 2 * rows), f32),
    ]
    if second:
        outs += [shape((rows, width))]
    held, sems = weight_scratch(layout, 1, width, True)
    return run(
        functools.partial(heads_backward_kernel, second, layout), "heads_backward", 20, inputs, outs,
        held + [pltpu.VMEM((rows, width), bf16), pltpu.VMEM((heads, rows, rows), bf16)]
        + [pltpu.SemaphoreType.DMA((heads // 2,))] + sems, core, weights, after,
    )


def run_input_backward(second, layout, core, weights, inputs, slots, after):
    rows, width = inputs[0].shape
    outs = [shape((rows, width), f32), shape((1, width), f32)]
    if second:
        outs += [shape((rows, width)), shape((slots, width))]
    held, sems = weight_scratch(layout, 3, width, False)
    return run(
        functools.partial(input_backward_kernel, second, layout), "input_backward", 6, inputs, outs,
        held + sems, core, weights, after,
    )


def run_weight_backward(core, inputs, after):
    width = inputs[0].shape[1]
    outs = [shape((2, width, width))] * 2
    return run(weight_backward_kernel, "weight_backward", 6, inputs, outs, [], core, (), after)


def summed_blocks(pairs, little, device, devices, beside, after):
    bits = devices.bit_length() - 1
    _, tall, width = pairs[0].shape
    rows, step = tall // devices, width // pieces
    orders = [order[::-1] for order in bit_orders(bits)]
    me = device.astype(jnp.int32).reshape(1)
    if rows % 16:
        found = unfolded(
            jnp.concatenate(
                [(pairs[i].astype(f32) + pairs[i + 1].astype(f32)).astype(bf16) for i in (0, 2)]
            ),
            devices,
        )
        for at in range(bits):
            found = folded(found, at, device, devices)
            little = little + across(little, at, devices)
        sums = jnp.concatenate([p.reshape(4, rows, -1) for p in found], 2)
        return sums, little, [call(0) for call in beside]
    half = devices // 2
    outs = [shape((4, half, rows, step))] * (2 * pieces)
    found = run(
        functools.partial(fold_first_kernel, orders), "fold_first", 4, pairs, outs, [], me, (), after
    )
    results = []
    for at in range(bits):
        token, found = found[0], found[1:]
        after = ()
        if at < len(beside):
            after = (beside[at](token[0]),)
            results.extend(after)
        keeps = found[:pieces]
        gots = [across(found[pieces + p], orders[p][at], devices) for p in range(pieces)]
        little = little + token.astype(f32)
        little = little + across(little, at, devices)
        half //= 2
        if half:
            outs = [shape((4, half, rows, step))] * (2 * pieces)
            found = run(fold_kernel, "fold", 2, [*keeps, *gots], outs, [], me, (), after)
        else:
            outs = [shape((4, rows, width), f32)]
            found = run(fold_last_kernel, "fold_last", 1, [*keeps, *gots], outs, [], me)
    return found[1], little, results


def run_expert(kernel, mine, tall, middles, ups, downs, n_middle, us, name, after=()):
    slots, width = tall.shape
    inner = ups[0].shape[1]
    tiles = 6 if inner % 768 == 0 else 1
    tile = inner // tiles
    whole = pl.BlockSpec((slots, width), lambda j: (0, 0))
    part = pl.BlockSpec((slots, tile), lambda j: (0, j))

    def marked(*refs):
        at = 6 + len(middles)
        return kernel(*refs[:at], *refs[at + len(after) :])

    return pl.pallas_call(
        marked,
        grid=(tiles,),
        out_shape=[shape((slots, inner))] * n_middle + [shape((slots, width))],
        in_specs=[smem, whole] + [part] * len(middles) + [anywhere] * (4 + len(after)),
        out_specs=[part] * n_middle + [whole],
        scratch_shapes=[
            pltpu.VMEM((tiles, width, tile), bf16),
            pltpu.VMEM((tiles, tile, width), bf16),
            pltpu.VMEM((slots, width), f32),
            pltpu.SemaphoreType.DMA((2, tiles)),
        ],
        compiler_params=params(),
        cost_estimate=cost(us),
        name=name,
    )(mine, tall, *middles, *ups, *downs, *after)


def run_up_grad(buf_a, buf_b, dpre_a, dpre_b):
    slots, width = buf_a.shape
    inner = dpre_a.shape[1]
    tile = inner // 6
    whole = pl.BlockSpec((slots, width), lambda j: (0, 0))
    part = pl.BlockSpec((slots, tile), lambda j: (0, j))
    return pl.pallas_call(
        up_grad_kernel,
        grid=(6,),
        out_shape=shape((width, inner), f32),
        in_specs=[whole, whole, part, part],
        out_specs=pl.BlockSpec((width, tile), lambda j: (0, j)),
        compiler_params=params(),
        cost_estimate=cost(10),
        name="up_gradient",
    )(buf_a, buf_b, dpre_a, dpre_b)


def run_down_grad(dout_a, dout_b, act_a, act_b):
    slots, width = dout_a.shape
    inner = act_a.shape[1]
    tile = inner // 6
    whole = pl.BlockSpec((slots, width), lambda j: (0, 0))
    part = pl.BlockSpec((slots, tile), lambda j: (0, j))
    return pl.pallas_call(
        down_grad_kernel,
        grid=(6,),
        out_shape=shape((inner, width), f32),
        in_specs=[whole, whole, part, part],
        out_specs=pl.BlockSpec((tile, width), lambda j: (j, 0)),
        compiler_params=params(),
        cost_estimate=cost(10),
        name="down_gradient",
    )(dout_a, dout_b, act_a, act_b)


def swap(block):
    return lax.ppermute(block, "section", [(0, 1), (1, 0)])


def moved(block, source):
    return lax.ppermute(block, "section", [(source, 1 - source)])


def across(block, bit, devices):
    return lax.ppermute(block, "expert", [(i, i ^ (1 << bit)) for i in range(devices)])


def bit_orders(bits):
    if bits == 4:
        return [(3, 2, 0, 1), (3, 0, 1, 2), (3, 1, 2, 0)]
    names = list(range(bits))
    return [tuple(names[(i + r * bits // pieces) % bits] for i in names) for r in range(pieces)]


def split_lanes(block):
    step = block.shape[-1] // pieces
    return [block[..., p * step : (p + 1) * step] for p in range(pieces)]


def token_of(block):
    value = block[(0,) * block.ndim]
    return (value != value).astype(jnp.int32)


def gathered(shards, device, devices, after):
    bits = devices.bit_length() - 1
    orders = bit_orders(bits)
    rows = shards[0].shape[1]
    if rows % 16:
        found = [p.reshape(p.shape[:1] + (1,) * bits + p.shape[1:]) for p in shards]
        for step in range(bits):
            for p in range(pieces):
                bit = orders[p][step]
                axis = bits - bit
                got = across(found[p], bit, devices)
                high = (device >> bit) & 1 == 1
                found[p] = jnp.where(
                    high,
                    jnp.concatenate([got, found[p]], axis),
                    jnp.concatenate([found[p], got], axis),
                )
        found = [p.reshape(1, p.shape[0], -1, p.shape[-1]) for p in found]
        passed = [[moved(p, source) for p in found] for source in range(2)]
        return [[[0]]] * pieces, False, [[*found, *other] for other in passed]
    me = device.astype(jnp.int32).reshape(1)
    found = [p[None] for p in shards]
    differ = [[0] for _ in shards]
    for step in range(bits - 1):
        gots = [across(found[p], orders[p][step], devices) for p in range(pieces)]
        outs = [shape((2 * p.shape[0],) + p.shape[1:]) for p in found]
        last = after if step == bits - 2 else ()
        found = run(join_kernel, "join", 3, [*found, *gots], outs, [], me, (), last)[1:]
        for p in range(pieces):
            differ[p] = differ[p] + [d ^ (1 << orders[p][step]) for d in differ[p]]
    far = [across(found[p], orders[p][-1], devices) for p in range(pieces)]
    layout = [
        [differ[p], [d ^ (1 << orders[p][-1]) for d in differ[p]]] for p in range(pieces)
    ]
    own = [block for couple in zip(found, far) for block in couple]
    arrays = [[*own, *[moved(block, source) for block in own]] for source in range(2)]
    return layout, True, arrays


def halved(block, bit, bits, lead, device, devices, late=0):
    axis = lead + bits - 1 - bit
    low = lax.index_in_dim(block, 0, axis, keepdims=True)
    high = lax.index_in_dim(block, 1, axis, keepdims=True)
    got = across(jnp.where((device >> bit) & 1 == 1, low, high), bit, devices)
    up = ((device + late) >> bit) & 1 == 1
    return jnp.where(up, high, low).astype(f32) + got.astype(f32)


def folded(found, step, device, devices, late=0):
    bits = devices.bit_length() - 1
    orders = [order[::-1] for order in bit_orders(bits)]
    results = []
    for p in range(pieces):
        value = halved(found[p], orders[p][step], bits, 1, device, devices, late)
        results.append(value if step == bits - 1 else value.astype(bf16))
    return results


def unfolded(total, devices):
    bits = devices.bit_length() - 1
    return [
        p.reshape(p.shape[:1] + (2,) * bits + (p.shape[1] // devices, p.shape[2]))
        for p in split_lanes(total)
    ]


def body(
    block_input,
    cotangent,
    lengths,
    routes,
    norm_gain,
    attention_in,
    attention_out,
    position_bias,
    router,
    expert_up,
    expert_down,
):
    _, rows, width = block_input.shape
    section = lax.axis_index("section")
    device = lax.axis_index("expert")
    devices = lax.axis_size("expert")
    bits = devices.bit_length() - 1
    first = section == 0
    mine = [(section == which).astype(jnp.int32).reshape(1) for which in range(2)]
    experts = router.shape[2]
    shard_rows = router.shape[1]
    buckets, heads = position_bias.shape[1:]
    capacity = max(2, 3 * rows // (2 * experts))
    capacity = -(-capacity // 8) * 8
    slots = experts * capacity

    def both(own, other):
        return (jnp.where(first, own, other), jnp.where(first, other, own))

    def own_micro(block):
        return jnp.where(first, block[0], block[1])

    def other_micro(block):
        return jnp.where(first, block[1], block[0])

    own_shards = jnp.concatenate([attention_in[0], attention_out], axis=0)
    cut = split_lanes(own_shards)
    pad = cut[0].shape[-1] - experts
    cut[0] = jnp.concatenate([cut[0], jnp.pad(router, ((0, 0), (0, 0), (0, pad)))], axis=0)
    small_parts = (
        norm_gain[0].reshape(-1),
        position_bias[0].reshape(-1),
        other_micro(routes[0])[:, 0].astype(f32),
    )
    small = jnp.concatenate(small_parts)
    small = jnp.pad(small, (0, -small.shape[0] % 128)).reshape(-1, 128)
    small_given = swap(small).reshape(-1)
    split_at, at = [], 0
    for part in small_parts:
        at += part.shape[0]
        split_at.append(at)
    gain_other, table_other, route_other, _ = jnp.split(small_given, split_at)
    gains = both(norm_gain[0], gain_other.reshape(2, width))
    tables = both(position_bias[0], table_other.reshape(buckets, heads))
    route_pair = both(own_micro(routes[0])[:, 0], route_other.astype(jnp.int32))

    positions = jnp.arange(rows, dtype=jnp.int32)
    bounds = jnp.cumsum(own_micro(lengths)[0])
    segment = jnp.sum((positions[:, None] >= bounds[None, :]).astype(jnp.int32), axis=1)
    seg_col, seg_row = segment[:, None], segment[None, :]
    offsets = jnp.arange(2 * rows, dtype=jnp.int32) - (rows - 1)
    bucket_hot = (
        bucket_of(offsets)[:, None] == jnp.arange(buckets, dtype=jnp.int32)[None, :]
    ).astype(f32)
    lines = [
        lax.dot_general(table, bucket_hot, (((0,), (1,)), ((), ())), precision=highest)
        for table in tables
    ]
    bases = [run_bias(line, rows) for line in lines]
    before = (positions[:, None] > positions[None, :]).astype(bf16)
    places = []
    for route in route_pair:
        chosen = route[:, None] == jnp.arange(experts, dtype=jnp.int32)[None, :]
        earlier = dot(before, chosen.astype(bf16))
        slot = jnp.sum(jnp.where(chosen, earlier, 0.0), axis=1).astype(jnp.int32)
        places.append(route * capacity + slot)
    route_cols = [route[:, None] for route in route_pair]
    place_cols = [place[:, None] for place in places]
    place_rows = [place[None, :] for place in places]
    layout, apart, weights = gathered(
        cut, device, devices, (place_rows[0], route_cols[0], seg_col, seg_row, gains[0])
    )
    core = jnp.stack([section, device if apart else jnp.zeros_like(device)]).astype(jnp.int32)
    up_other = swap(expert_up[0, 0])
    down_other = swap(expert_down[0, 0])
    ups, downs = (expert_up[0, 0], up_other), (expert_down[0, 0], down_other)

    def exchanged(block):
        return lax.all_to_all(block, "expert", split_axis=0, concat_axis=0, tiled=True)

    def expert_forward(which, arrived):
        return run_expert(
            expert_forward_kernel, mine[which], arrived, (), ups, downs, 2, 11, "expert_forward",
            weights[1][len(weights[1]) // 2 :] if which == 0 else (),
        )

    def expert_backward(mine, arrived, slope):
        return run_expert(
            expert_backward_kernel, mine, arrived, (slope,), ups, downs, 1, 11,
            "expert_backward",
        )

    def shared_inputs(which):
        return (
            gains[which], seg_col, seg_row, route_cols[which],
        )

    inputs = own_micro(block_input)
    cot = own_micro(cotangent)
    token, q0, k0, v0, o0, p0, mid0, h20, share0, gate0, send0 = run_forward(
        False, layout, core, [*weights[0], bases[0]], (inputs, *shared_inputs(0), place_rows[0]), slots, experts,
        heads, (),
    )
    buf0 = exchanged(send0)
    act0, slope0, result0 = expert_forward(0, buf0)
    back0 = exchanged(result0)
    _, q1, k1, v1, o1, p1, mid1, h21, share1, gate1, send1, between, combined0, grad_send1 = (
        run_forward(
            True, layout, core, [*weights[1], bases[1]],
            (mid0, gate0, place_cols[0], back0, cot, *shared_inputs(1), place_rows[1]),
            slots, experts, heads, (),
        )
    )
    buf1 = exchanged(send1)
    dout1 = exchanged(grad_send1)
    act1, slope1, result1 = expert_forward(1, buf1)
    dpre1, dbuf1 = expert_backward(mine[1], dout1, slope1)
    back1 = exchanged(
        jnp.concatenate(
            [block.reshape(experts, capacity, width) for block in (result1, dbuf1)], axis=1
        ).reshape(2 * slots, width)
    )
    place_out = place_cols[1] + route_cols[1] * capacity
    _, dx11, low1, dq1, dk1, dv1, router_grad1, gain_two1, line_grad1, last = run_heads_backward(
        True, layout, core, [*weights[1], p1],
        (q1, k1, v1, mid1, h21, share1, gate1, cot, back1, place_out, gains[1],
         route_cols[1], place_out + capacity),
        experts, (),
    )
    token, dx1, gain_one1, dy0, grad_send0 = run_input_backward(
        True, layout, core, weights[1],
        (between, dx11, dq1, dk1, dv1, gains[1], gate0, place_rows[0]), slots, (),
    )
    token, keep1, give1 = run_weight_backward(
        core + token[0], (between, gains[1], o1, low1, dq1, dk1, dv1), ()
    )
    dout0 = exchanged(grad_send0)

    given1 = swap(give1)
    dpre0, dbuf0 = expert_backward(mine[0] + token[0], dout0, slope0)
    dback0 = exchanged(dbuf0)
    from_first = [swap(block) for block in (buf1, act1, dout1, dpre1)]
    from_second = [swap(block) for block in (buf0, act0, dout0, dpre0)]

    def up_of(bufs, dpres):
        return run_up_grad(*bufs, *dpres)

    def down_of(douts, acts):
        return run_down_grad(*douts, *acts)

    up_sets = ((buf0, from_second[0], dpre0, from_second[3]), (buf1, from_first[0], dpre1, from_first[3]))
    down_sets = ((dout0, from_second[2], act0, from_second[1]), (dout1, from_first[2], act1, from_first[1]))

    def own_layer(run_grad, sets, token):
        return lax.cond(
            section + token == 0, lambda a, b: run_grad(*a), lambda a, b: run_grad(*b), *sets
        )

    grads = [
        functools.partial(own_layer, run_down_grad, down_sets),
        functools.partial(own_layer, run_up_grad, up_sets),
    ]

    grad_down = grads[0](token_of(dbuf0))
    token, dx10, low0, dq0, dk0, dv0, router_grad0, gain_two0, line_grad0 = run_heads_backward(
        False, layout, core, [*weights[0], p0],
        (q0, k0, v0, mid0, h20, share0, gate0, dy0, dback0, combined0, gains[0],
         route_cols[0], place_cols[0]),
        experts, (grad_down,),
    )
    token, keep0, give0 = run_weight_backward(
        core, (inputs, gains[0], o0, low0, dq0, dk0, dv0), ()
    )
    _, dx0, gain_one0 = run_input_backward(
        False, layout, core + token[0], weights[0], (inputs, dx10, dq0, dk0, dv0, gains[0]), slots, ()
    )

    little = [
        jnp.concatenate(parts, axis=0)
        for parts in (
            (gain_one0, gain_two0, line_grad0, router_grad0),
            (gain_one1, gain_two1, line_grad1, router_grad1),
        )
    ]
    little = jnp.where(first, little[0], little[1]) + swap(jnp.where(first, little[1], little[0]))
    sums, little_sum, (grad_up,) = summed_blocks(
        [keep0, swap(give0), keep1, given1], little, device, devices, grads[1:], (dx0,)
    )
    shared0, shared1 = sums[:2], sums[2:]
    shared_other = swap(jnp.where(first, shared1, shared0))
    queries_keys = jnp.where(first, shared0, shared_other)
    values_out = jnp.where(first, shared_other, shared1)

    grad_table = jnp.dot(little_sum[2 : 2 + heads], bucket_hot, precision=highest).T
    router_sum = lax.dynamic_slice_in_dim(little_sum[2 + heads :], device * shard_rows, shard_rows, 1)

    out_other = swap(jnp.where(first, last, between))
    layer_out = jnp.stack(
        [jnp.where(first, between, out_other), jnp.where(first, out_other, last)]
    )
    grad_other = swap(jnp.where(first, dx1, dx0))
    input_grad = jnp.stack([jnp.where(first, dx0, grad_other), jnp.where(first, grad_other, dx1)])
    return (
        layer_out[None],
        input_grad[None],
        little_sum[:2][None],
        jnp.concatenate([queries_keys, values_out[:1]], axis=0)[None],
        values_out[1][None],
        grad_table[None],
        router_sum.T[None],
        grad_up[None, None],
        grad_down[None, None],
    )


def solution(mesh):
    in_specs = (
        P(None, "expert", None),
        P(None, "expert", None),
        P(None, "expert", None),
        P("section", None, "expert", None),
        P("section", None, None),
        P("section", None, "expert", None),
        P("section", "expert", None),
        P("section", None, None),
        P("section", "expert", None),
        P("section", "expert", None, None),
        P("section", "expert", None, None),
    )
    out_specs = (
        P("section", None, "expert", None),
        P("section", None, "expert", None),
        P("section", None, None),
        P("section", None, "expert", None),
        P("section", "expert", None),
        P("section", None, None),
        P("section", "expert", None),
        P("section", "expert", None, None),
        P("section", "expert", None, None),
    )
    return jax.shard_map(body, mesh=mesh, in_specs=in_specs, out_specs=out_specs, check_vma=False)
```

```python
import functools

import jax
import jax.numpy as jnp
from jax import lax
from jax.experimental import pallas as pl
from jax.experimental.pallas import tpu as pltpu
from jax.sharding import PartitionSpec as P

bucket_edges = (12, 16, 23, 32, 46, 64, 91)
norm_eps = 1e-06
gelu_c = 0.7978845608028654
gelu_cube = 0.044715
masked_score = -1e30
highest = lax.Precision.HIGHEST
f32 = jnp.float32
bf16 = jnp.bfloat16
vmem_bytes = 56 * 2**20
small_bytes = 22 * 2**20
small_kernels = ("fold_first", "fold", "fold_last", "join")
pieces = 3


def dot(left, right):
    return jnp.dot(left, right, preferred_element_type=f32)


def dot_lead(left, right):
    return lax.dot_general(left, right, (((0,), (0,)), ((), ())), preferred_element_type=f32)


def dot_last(left, right):
    return lax.dot_general(left, right, (((1,), (1,)), ((), ())), preferred_element_type=f32)


def gelu_pair(value):
    square = value * value
    inner = jnp.tanh(gelu_c * value * (1.0 + gelu_cube * square))
    half = 0.5 * (1.0 + inner)
    slope = half + 0.5 * value * (1.0 - inner * inner) * (
        gelu_c * (1.0 + 3.0 * gelu_cube * square)
    )
    return (value * half, slope)


def bucket_of(offset):
    distance = jnp.abs(offset)
    found = 16 * (offset > 0).astype(jnp.int32) + jnp.minimum(distance, 8)
    for edge in bucket_edges:
        found = found + (distance >= edge).astype(jnp.int32)
    return found


def norm_scale(values):
    return lax.rsqrt(jnp.mean(values * values, axis=-1, keepdims=True) + norm_eps)


def norm_backward(values, gain, grad_normed):
    scale = norm_scale(values)
    normal = values * scale
    inner = grad_normed * gain
    grad_values = scale * (inner - normal * jnp.mean(inner * normal, axis=-1, keepdims=True))
    return (grad_values, jnp.sum(grad_normed * normal, axis=0, keepdims=True))


def zero_token(token_ref):
    token_ref[0] = 0


def weight_copies(place_ref, layer, matrices, blocks, weights, router, sems):
    core, device = place_ref[0], place_ref[1]
    first, count = matrices
    copies = []
    for p in range(pieces):
        for (here, differ), (there, _) in zip(blocks[0][p], blocks[1][p]):
            rows, step = here.shape[2:]
            for at in range(here.shape[0]):
                target = pl.ds(pl.multiple_of((device ^ differ[at]) * rows, rows), rows)
                couples = [
                    (pl.ds(first, count), pl.ds(0, step), weights.at[:, target, pl.ds(p * step, step)])
                ]
                if p == 0 and router is not None:
                    couples.append((4, pl.ds(0, 128), router.at[target, :]))
                for which, lanes, goal in couples:
                    sem = sems.at[len(copies)]
                    own = pltpu.make_async_copy(here.at[at, which, :, lanes], goal, sem)
                    other = pltpu.make_async_copy(there.at[at, which, :, lanes], goal, sem)
                    copies.append(own)
                    pl.when(core == layer)(own.start)
                    pl.when(core != layer)(other.start)
    return copies


def laid_out(layout, refs):
    blocks, at = [], 0
    for _ in range(2):
        blocks.append([])
        for piece in layout:
            blocks[-1].append([(refs[at + i], differ) for i, differ in enumerate(piece)])
            at += len(piece)
    return blocks, refs[at:]


def join_kernel(place_ref, *refs):
    olds, gots, outs = refs[:pieces], refs[pieces : 2 * pieces], refs[2 * pieces :]
    token_ref, outs = outs[0], outs[1:]
    zero_token(token_ref)
    for old, got, out in zip(olds, gots, outs):
        half = old.shape[0]
        out[:half] = old[...]
        out[half:] = got[...]


def head_masks():
    lane = lax.broadcasted_iota(jnp.int32, (1, 128), 1)
    low = (lane < 64).astype(f32)
    return (low.astype(bf16), (1.0 - low).astype(bf16))


def bias_kernel(line_ref, base_ref):
    heads, _, reach = base_ref.shape
    wide = line_ref.shape[1]

    def one(head, carry):
        line = jnp.broadcast_to(line_ref[pl.ds(head, 1), :], (128, wide))
        turned = pltpu.roll(line, wide - 127, 1, stride=1, stride_axis=0)
        base_ref[head] = turned[:, :reach]
        return carry

    lax.fori_loop(0, heads, one, 0)


def bias_of(base_ref, head, rows):
    blocks = rows // 128
    return jnp.concatenate(
        [base_ref[head, :, 128 * (blocks - 1 - a) : 128 * (blocks - 1 - a) + rows] for a in range(blocks)],
        axis=0,
    )


def diagonal_line(grad_scores, flip, wide):
    blocks = grad_scores.shape[0] // 128
    parts = [None] * (wide // 128)
    for a in range(blocks):
        flipped = dot(flip, grad_scores[128 * a : 128 * (a + 1), :])
        for j in range(blocks):
            piece = flipped[:, 128 * j : 128 * (j + 1)]
            at = j + blocks - 1 - a
            parts[at] = piece if parts[at] is None else parts[at] + piece
    empty = jnp.zeros((128, 128), f32)
    sums = jnp.concatenate([empty if part is None else part for part in parts], axis=1)
    turned = pltpu.roll(sums, 0, 1, stride=1, stride_axis=0)
    return jnp.sum(turned, axis=0, keepdims=True)


def one_hot_columns(place_col, slots):
    rows = place_col.shape[0]
    return (place_col == lax.broadcasted_iota(jnp.int32, (rows, slots), 1)).astype(f32).astype(bf16)


def one_hot_rows(place_row, slots):
    rows = place_row.shape[1]
    return (place_row == lax.broadcasted_iota(jnp.int32, (slots, rows), 0)).astype(f32).astype(bf16)


def forward_kernel(second, experts, layout, core_ref, *refs):
    blocks, refs = laid_out(layout, refs)
    base_hbm, refs = refs[0], refs[1:]
    if second:
        (before_ref, gate_before_ref, place_before_ref, back_ref, cot_ref), refs = refs[:5], refs[5:]
    else:
        (x_ref,), refs = refs[:1], refs[1:]
    (gain_ref, seg_col_ref, seg_row_ref, route_ref, place_ref), refs = refs[:5], refs[5:]
    (
        token_ref, q_ref, k_ref, v_ref, o_ref, p_hbm, mid_ref, h2_ref, share_ref, gate_ref, send_ref,
    ), refs = refs[:11], refs[11:]
    if second:
        (x_out_ref, combined_ref, grad_send_ref), refs = refs[:3], refs[3:]
    weights, router_ref, mask_ref, base_ref, p_ref, part_sems, sems = refs
    zero_token(token_ref)
    copies = weight_copies(core_ref, int(second), (0, 4), blocks, weights, router_ref, sems)
    base_copy = pltpu.make_async_copy(base_hbm, base_ref, part_sems.at[0])
    base_copy.start()
    slots = send_ref.shape[0]
    rows = q_ref.shape[0]
    if second:
        scatter = one_hot_columns(place_before_ref[...], slots)
        combined = dot(scatter, back_ref[...])
        combined_ref[...] = combined.astype(bf16)
        low = (before_ref[...] + gate_before_ref[...] * combined).astype(bf16)
        x_out_ref[...] = low
        wide = low.astype(f32)
    else:
        wide = x_ref[...].astype(f32)
    h1 = (wide * norm_scale(wide) * gain_ref[0:1, :]).astype(bf16)
    mask_ref[...] = jnp.where(seg_col_ref[...] == seg_row_ref[...], 0.0, masked_score)
    for copy in copies:
        copy.wait()
    q_ref[...] = dot(h1, weights[0]).astype(bf16)
    k_ref[...] = dot(h1, weights[1]).astype(bf16)
    v_ref[...] = dot(h1, weights[2]).astype(bf16)
    masks = head_masks()
    base_copy.wait()

    def leaving(p):
        both = pl.ds(2 * p, 2)
        return pltpu.make_async_copy(p_ref.at[both], p_hbm.at[both], part_sems.at[1 + p])

    def pair(p, carry):
        columns = pl.ds(pl.multiple_of(p * 128, 128), 128)
        queries, keys, values = q_ref[:, columns], k_ref[:, columns], v_ref[:, columns]
        mixed = jnp.zeros((rows, 128), f32)
        for half in range(2):
            head = 2 * p + half
            scores = dot_last(queries * masks[half], keys) * 0.125 + bias_of(base_ref, head, rows)
            scores = scores + mask_ref[...]
            raised = jnp.exp(scores - jnp.max(scores, axis=-1, keepdims=True))
            total = jnp.sum(raised, axis=-1, keepdims=True)
            shares = (raised * (1.0 / total)).astype(bf16)
            p_ref[head] = shares
            mixed = mixed + dot(shares, values * masks[half])
        o_ref[:, columns] = mixed.astype(bf16)
        leaving(p).start()
        return carry

    lax.fori_loop(0, p_ref.shape[0] // 2, pair, 0)
    middle = wide + dot(o_ref[...], weights[3])
    mid_ref[...] = middle
    h2 = (middle * norm_scale(middle) * gain_ref[1:2, :]).astype(bf16)
    h2_ref[...] = h2
    logits = dot(h2, router_ref[...])
    lane = lax.broadcasted_iota(jnp.int32, (1, 128), 1)
    logits = jnp.where(lane < experts, logits, masked_score)
    raised = jnp.exp(logits - jnp.max(logits, axis=-1, keepdims=True))
    shares = raised / jnp.sum(raised, axis=-1, keepdims=True)
    share_ref[...] = shares
    chosen = route_ref[...] == lax.broadcasted_iota(jnp.int32, shares.shape, 1)
    gate = jnp.sum(jnp.where(chosen, shares, 0.0), axis=-1, keepdims=True)
    gate_ref[...] = gate
    gather = one_hot_rows(place_ref[...], slots)
    send_ref[...] = dot(gather, h2).astype(bf16)
    if second:
        grad_out = (gate * cot_ref[...].astype(f32)).astype(bf16)
        grad_send_ref[...] = dot(gather, grad_out).astype(bf16)
    for p in range(p_ref.shape[0] // 2):
        leaving(p).wait()


def heads_backward_kernel(second, layout, core_ref, *refs):
    blocks, refs = laid_out(layout, refs)
    p_hbm, refs = refs[0], refs[1:]
    (
        q_ref, k_ref, v_ref, mid_ref, h2_ref, share_ref, gate_ref, dy_ref, dback_ref,
        out_ref, gain_ref, route_ref, place_ref,
    ), refs = refs[:13], refs[13:]
    (
        token_ref, dx1_ref, low_ref, dq_ref, dk_ref, dv_ref, router_grad_ref, gain_grad_ref,
        line_grad_ref,
    ), refs = refs[:9], refs[9:]
    if second:
        (y_ref,), refs = refs[:1], refs[1:]
    weights, router_ref, do_ref, p_ref, part_sems, sems = refs
    zero_token(token_ref)

    def arriving(p):
        both = pl.ds(2 * p, 2)
        return pltpu.make_async_copy(p_hbm.at[both], p_ref.at[both], part_sems.at[p])

    copies = weight_copies(core_ref, int(second), (3, 1), blocks, weights, router_ref, sems)
    for p in range(p_ref.shape[0] // 2):
        arriving(p).start()
    rows = q_ref.shape[0]
    slots = dback_ref.shape[0]
    dy = dy_ref[...].astype(f32)
    gate = gate_ref[...]
    middle = mid_ref[...]
    scatter = one_hot_columns(place_ref[...], slots)
    if second:
        combined = dot(one_hot_columns(out_ref[...], slots), dback_ref[...])
        y_ref[...] = (middle + gate * combined).astype(bf16)
    else:
        combined = out_ref[...].astype(f32)
    grad_gate = jnp.sum(dy * combined, axis=-1, keepdims=True)
    shares = share_ref[...]
    chosen = route_ref[...] == lax.broadcasted_iota(jnp.int32, shares.shape, 1)
    grad_logits = (grad_gate * gate * (chosen.astype(f32) - shares)).astype(bf16)
    router_grad_ref[...] = dot_lead(grad_logits, h2_ref[...])[: router_grad_ref.shape[0]]
    for copy in copies:
        copy.wait()
    grad_two = dot(scatter, dback_ref[...]) + dot_last(grad_logits, router_ref[...])
    grad_middle, gain_two = norm_backward(middle, gain_ref[1:2, :], grad_two)
    gain_grad_ref[...] = gain_two
    grad_middle = grad_middle + dy
    dx1_ref[...] = grad_middle
    low = grad_middle.astype(bf16)
    low_ref[...] = low
    do_ref[...] = dot_last(low, weights[0]).astype(bf16)
    masks = head_masks()
    flip = (
        lax.broadcasted_iota(jnp.int32, (128, 128), 0)
        + lax.broadcasted_iota(jnp.int32, (128, 128), 1)
        == 127
    )
    flip = flip.astype(f32).astype(bf16)

    def pair(p, carry):
        arriving(p).wait()
        columns = pl.ds(pl.multiple_of(p * 128, 128), 128)
        queries, keys, values = q_ref[:, columns], k_ref[:, columns], v_ref[:, columns]
        grad_mixed = do_ref[:, columns]
        dq = jnp.zeros((rows, 128), f32)
        dk = jnp.zeros((rows, 128), f32)
        dv = jnp.zeros((rows, 128), f32)
        for half in range(2):
            head = 2 * p + half
            own_mixed = grad_mixed * masks[half]
            low_shares = p_ref[head]
            shares = low_shares.astype(f32)
            grad_shares = dot_last(own_mixed, values)
            mean = jnp.sum(shares * grad_shares, axis=-1, keepdims=True)
            grad_scores = (shares * (grad_shares - mean)).astype(bf16)
            dv = dv + dot_lead(low_shares, own_mixed)
            dq = dq + dot(grad_scores, keys * masks[half])
            dk = dk + dot_lead(grad_scores, queries * masks[half])
            line_grad_ref[pl.ds(head, 1), :] = diagonal_line(
                grad_scores, flip, line_grad_ref.shape[1]
            )
        dq_ref[:, columns] = (dq * 0.125).astype(bf16)
        dk_ref[:, columns] = (dk * 0.125).astype(bf16)
        dv_ref[:, columns] = dv.astype(bf16)
        return carry

    lax.fori_loop(0, p_ref.shape[0] // 2, pair, 0)


def input_backward_kernel(second, layout, core_ref, *refs):
    blocks, refs = laid_out(layout, refs)
    (x_ref, dx1_ref, dq_ref, dk_ref, dv_ref, gain_ref), refs = refs[:6], refs[6:]
    if second:
        (gate_next_ref, place_next_ref), refs = refs[:2], refs[2:]
    (token_ref, dx_ref, gain_grad_ref), refs = refs[:3], refs[3:]
    if second:
        (low_out_ref, grad_send_ref), refs = refs[:2], refs[2:]
    weights, sems = refs
    zero_token(token_ref)
    copies = weight_copies(core_ref, int(second), (0, 3), blocks, weights, None, sems)
    for copy in copies:
        copy.wait()
    wide = x_ref[...].astype(f32)
    grad_one = (
        dot_last(dq_ref[...], weights[0])
        + dot_last(dk_ref[...], weights[1])
        + dot_last(dv_ref[...], weights[2])
    )
    grad_inputs, gain_one = norm_backward(wide, gain_ref[0:1, :], grad_one)
    grad_inputs = grad_inputs + dx1_ref[...]
    dx_ref[...] = grad_inputs
    gain_grad_ref[...] = gain_one
    if second:
        low = grad_inputs.astype(bf16)
        low_out_ref[...] = low
        grad_out = (gate_next_ref[...] * low.astype(f32)).astype(bf16)
        gather = one_hot_rows(place_next_ref[...], grad_send_ref.shape[0])
        grad_send_ref[...] = dot(gather, grad_out).astype(bf16)


def weight_backward_kernel(core_ref, x_ref, gain_ref, o_ref, low_ref, dq_ref, dk_ref, dv_ref, *refs):
    token_ref, keep_ref, give_ref = refs
    zero_token(token_ref)
    core = core_ref[0]

    def put(matrix, value):
        value = value.astype(bf16)

        @pl.when(core == matrix // 2)
        def _():
            keep_ref[matrix % 2] = value

        @pl.when(core != matrix // 2)
        def _():
            give_ref[matrix % 2] = value

    wide = x_ref[...].astype(f32)
    h1 = (wide * norm_scale(wide) * gain_ref[0:1, :]).astype(bf16)
    put(0, dot_lead(h1, dq_ref[...]))
    put(1, dot_lead(h1, dk_ref[...]))
    put(2, dot_lead(h1, dv_ref[...]))
    put(3, dot_lead(o_ref[...], low_ref[...]))


def places_of(block, order):
    place = 0
    for bit in order:
        place = 2 * place + ((block >> bit) & 1)
    return place


def fold_first_kernel(orders, device_ref, *refs):
    sums, outs = refs[:4], refs[4:]
    token_ref, outs = outs[0], outs[1:]
    zero_token(token_ref)
    keeps, sends = outs[:pieces], outs[pieces:]
    device = device_ref[0]
    half, rows, step = keeps[0].shape[1:]
    for block in range(2 * half):
        at = pl.ds(pl.multiple_of((device ^ block) * rows, rows), rows)
        for layer in range(2):
            for matrix in range(2):
                total = sums[2 * layer][matrix, at, :].astype(f32)
                total = (total + sums[2 * layer + 1][matrix, at, :].astype(f32)).astype(bf16)
                for p in range(pieces):
                    place = places_of(block, orders[p])
                    target = sends[p] if place >= half else keeps[p]
                    target[2 * layer + matrix, place % half] = total[:, p * step : (p + 1) * step]


def fold_kernel(device_ref, *refs):
    olds, gots, outs = refs[:pieces], refs[pieces : 2 * pieces], refs[2 * pieces :]
    token_ref, outs = outs[0], outs[1:]
    zero_token(token_ref)
    for p in range(pieces):
        total = olds[p][...].astype(f32) + gots[p][...].astype(f32)
        half = total.shape[1] // 2
        outs[p][...] = total[:, :half].astype(bf16)
        outs[pieces + p][...] = total[:, half:].astype(bf16)


def fold_last_kernel(device_ref, *refs):
    olds, gots, (token_ref, out_ref) = refs[:pieces], refs[pieces : 2 * pieces], refs[2 * pieces :]
    zero_token(token_ref)
    for p in range(pieces):
        step = olds[p].shape[3]
        total = olds[p][...].astype(f32) + gots[p][...].astype(f32)
        out_ref[:, :, p * step : (p + 1) * step] = total[:, 0]


def expert_copies(mine, tiles, up_refs, down_refs, up, down, sems, start):
    width = up.shape[2]

    def copies(which):
        found = []
        for j in range(tiles):
            at = pl.ds(j * width, width)
            found.append(
                (
                    pltpu.make_async_copy(up_refs[which].at[:, at], up.at[j], sems.at[0, j]),
                    pltpu.make_async_copy(down_refs[which].at[at, :], down.at[j], sems.at[1, j]),
                )
            )
        return found

    if start:
        for which in range(2):

            @pl.when(mine == 1 - which)
            def _():
                for couple in copies(which):
                    for copy in couple:
                        copy.start()


def expert_wait(j, up_ref, down_ref, up, down, sems):
    width = up.shape[2]
    at = pl.ds(0, width)
    pltpu.make_async_copy(up_ref.at[:, at], up.at[j], sems.at[0, j]).wait()
    pltpu.make_async_copy(down_ref.at[at, :], down.at[j], sems.at[1, j]).wait()


def expert_forward_kernel(
    mine_ref, x_ref, up_own, up_other, down_own, down_other, act_ref, slope_ref, out_ref,
    up, down, total, sems,
):
    j = pl.program_id(0)
    tiles = up.shape[0]

    @pl.when(j == 0)
    def _():
        expert_copies(
            mine_ref[0], tiles, (up_own, up_other), (down_own, down_other), up, down, sems, True
        )
        total[...] = jnp.zeros_like(total)

    expert_wait(j, up_own, down_own, up, down, sems)
    active, slope = gelu_pair(dot(x_ref[...], up[j]))
    active = active.astype(bf16)
    act_ref[...] = active
    slope_ref[...] = slope.astype(bf16)
    total[...] += dot(active, down[j])

    @pl.when(j == tiles - 1)
    def _():
        out_ref[...] = total[...].astype(bf16)


def expert_backward_kernel(
    mine_ref, dout_ref, slope_ref, up_own, up_other, down_own, down_other, dpre_ref, dbuf_ref,
    up, down, total, sems,
):
    j = pl.program_id(0)
    tiles = up.shape[0]

    @pl.when(j == 0)
    def _():
        expert_copies(
            mine_ref[0], tiles, (up_own, up_other), (down_own, down_other), up, down, sems, True
        )
        total[...] = jnp.zeros_like(total)

    expert_wait(j, up_own, down_own, up, down, sems)
    grad_pre = (dot_last(dout_ref[...], down[j]) * slope_ref[...].astype(f32)).astype(bf16)
    dpre_ref[...] = grad_pre
    total[...] += dot_last(grad_pre, up[j])

    @pl.when(j == tiles - 1)
    def _():
        dbuf_ref[...] = total[...].astype(bf16)


def up_grad_kernel(buf_a, buf_b, dpre_a, dpre_b, grad_ref):
    grad_ref[...] = dot_lead(buf_a[...], dpre_a[...]) + dot_lead(buf_b[...], dpre_b[...])


def down_grad_kernel(dout_a, dout_b, act_a, act_b, grad_ref):
    grad_ref[...] = dot_lead(act_a[...], dout_a[...]) + dot_lead(act_b[...], dout_b[...])


def shape(dims, kind=bf16):
    return jax.ShapeDtypeStruct(dims, kind)


def params(limit=vmem_bytes):
    return pltpu.CompilerParams(vmem_limit_bytes=limit)


def cost(us):
    return pl.CostEstimate(flops=int(us * 1e9), bytes_accessed=0, transcendentals=0)


smem = pl.BlockSpec(memory_space=pltpu.SMEM)
vmem = pl.BlockSpec(memory_space=pltpu.VMEM)
anywhere = pl.BlockSpec(memory_space=pl.ANY)
hbm = pl.BlockSpec(memory_space=pltpu.HBM)


def run(kernel, name, us, inputs, outs, scratch, core, weights=(), after=(), apart=()):
    def marked(core_ref, *refs):
        at = len(weights) + len(inputs)
        return kernel(core_ref, *refs[:at], *refs[at + len(after) :])

    outs = [shape((1,), jnp.int32)] + list(outs)
    return pl.pallas_call(
        marked,
        out_shape=outs,
        in_specs=[smem]
        + [anywhere] * len(weights)
        + [vmem] * len(inputs)
        + [anywhere] * len(after),
        out_specs=[smem] + [hbm if at in apart else vmem for at in range(len(outs) - 1)],
        scratch_shapes=scratch,
        compiler_params=params(small_bytes if name in small_kernels else vmem_bytes),
        cost_estimate=cost(us),
        name=name,
    )(core, *weights, *inputs, *after)


def weight_scratch(layout, count, width, router):
    copies = sum(len(differ) for piece in layout for differ in piece)
    held = [pltpu.VMEM((count, width, width), bf16)]
    if router:
        copies += sum(len(differ) for differ in layout[0])
        held.append(pltpu.VMEM((width, 128), bf16))
    return held, [pltpu.SemaphoreType.DMA((copies,))]


def run_bias(line, rows):
    heads, wide = line.shape
    return pl.pallas_call(
        bias_kernel,
        out_shape=shape((heads, 128, 2 * rows - 128), f32),
        in_specs=[vmem],
        out_specs=vmem,
        compiler_params=params(),
        cost_estimate=cost(3),
        name="bias_base",
    )(line)


def run_forward(second, layout, core, weights, inputs, slots, experts, heads, after):
    rows, width = inputs[0].shape
    outs = [shape((rows, width))] * 4 + [
        shape((heads, rows, rows)),
        shape((rows, width), f32),
        shape((rows, width)),
        shape((rows, 128), f32),
        shape((rows, 1), f32),
        shape((slots, width)),
    ]
    if second:
        outs += [shape((rows, width)), shape((rows, width)), shape((slots, width))]
    held, sems = weight_scratch(layout, 4, width, True)
    return run(
        functools.partial(forward_kernel, second, experts, layout), "attention_forward", 15, inputs, outs,
        held + [pltpu.VMEM((rows, rows), f32)]
        + [pltpu.VMEM((heads, 128, 2 * rows - 128), f32), pltpu.VMEM((heads, rows, rows), bf16)]
        + [pltpu.SemaphoreType.DMA((1 + heads // 2,))] + sems, core, weights, after, (4,),
    )


def run_heads_backward(second, layout, core, weights, inputs, experts, after):
    rows, width = inputs[0].shape
    heads = weights[-1].shape[0]
    outs = [shape((rows, width), f32)] + [shape((rows, width))] * 4 + [
        shape((experts, width), f32),
        shape((1, width), f32),
        shape((heads, 2 * rows), f32),
    ]
    if second:
        outs += [shape((rows, width))]
    held, sems = weight_scratch(layout, 1, width, True)
    return run(
        functools.partial(heads_backward_kernel, second, layout), "heads_backward", 20, inputs, outs,
        held + [pltpu.VMEM((rows, width), bf16), pltpu.VMEM((heads, rows, rows), bf16)]
        + [pltpu.SemaphoreType.DMA((heads // 2,))] + sems, core, weights, after,
    )


def run_input_backward(second, layout, core, weights, inputs, slots, after):
    rows, width = inputs[0].shape
    outs = [shape((rows, width), f32), shape((1, width), f32)]
    if second:
        outs += [shape((rows, width)), shape((slots, width))]
    held, sems = weight_scratch(layout, 3, width, False)
    return run(
        functools.partial(input_backward_kernel, second, layout), "input_backward", 6, inputs, outs,
        held + sems, core, weights, after,
    )


def run_weight_backward(core, inputs, after):
    width = inputs[0].shape[1]
    outs = [shape((2, width, width))] * 2
    return run(weight_backward_kernel, "weight_backward", 6, inputs, outs, [], core, (), after)


def summed_blocks(pairs, little, device, devices, beside, after):
    bits = devices.bit_length() - 1
    _, tall, width = pairs[0].shape
    rows, step = tall // devices, width // pieces
    orders = [order[::-1] for order in bit_orders(bits)]
    me = device.astype(jnp.int32).reshape(1)
    if rows % 16:
        found = unfolded(
            jnp.concatenate(
                [(pairs[i].astype(f32) + pairs[i + 1].astype(f32)).astype(bf16) for i in (0, 2)]
            ),
            devices,
        )
        for at in range(bits):
            found = folded(found, at, device, devices)
            little = little + across(little, at, devices)
        sums = jnp.concatenate([p.reshape(4, rows, -1) for p in found], 2)
        return sums, little, [call(0) for call in beside]
    half = devices // 2
    outs = [shape((4, half, rows, step))] * (2 * pieces)
    found = run(
        functools.partial(fold_first_kernel, orders), "fold_first", 4, pairs, outs, [], me, (), after
    )
    results = []
    for at in range(bits):
        token, found = found[0], found[1:]
        after = ()
        if at < len(beside):
            after = (beside[at](token[0]),)
            results.extend(after)
        keeps = found[:pieces]
        gots = [across(found[pieces + p], orders[p][at], devices) for p in range(pieces)]
        little = little + token.astype(f32)
        little = little + across(little, at, devices)
        half //= 2
        if half:
            outs = [shape((4, half, rows, step))] * (2 * pieces)
            found = run(fold_kernel, "fold", 2, [*keeps, *gots], outs, [], me, (), after)
        else:
            outs = [shape((4, rows, width), f32)]
            found = run(fold_last_kernel, "fold_last", 1, [*keeps, *gots], outs, [], me)
    return found[1], little, results


def run_expert(kernel, mine, tall, middles, ups, downs, n_middle, us, name, after=()):
    slots, width = tall.shape
    inner = ups[0].shape[1]
    tiles = 6 if inner % 768 == 0 else 1
    tile = inner // tiles
    whole = pl.BlockSpec((slots, width), lambda j: (0, 0))
    part = pl.BlockSpec((slots, tile), lambda j: (0, j))

    def marked(*refs):
        at = 6 + len(middles)
        return kernel(*refs[:at], *refs[at + len(after) :])

    return pl.pallas_call(
        marked,
        grid=(tiles,),
        out_shape=[shape((slots, inner))] * n_middle + [shape((slots, width))],
        in_specs=[smem, whole] + [part] * len(middles) + [anywhere] * (4 + len(after)),
        out_specs=[part] * n_middle + [whole],
        scratch_shapes=[
            pltpu.VMEM((tiles, width, tile), bf16),
            pltpu.VMEM((tiles, tile, width), bf16),
            pltpu.VMEM((slots, width), f32),
            pltpu.SemaphoreType.DMA((2, tiles)),
        ],
        compiler_params=params(),
        cost_estimate=cost(us),
        name=name,
    )(mine, tall, *middles, *ups, *downs, *after)


def run_up_grad(buf_a, buf_b, dpre_a, dpre_b):
    slots, width = buf_a.shape
    inner = dpre_a.shape[1]
    tile = inner // 6
    whole = pl.BlockSpec((slots, width), lambda j: (0, 0))
    part = pl.BlockSpec((slots, tile), lambda j: (0, j))
    return pl.pallas_call(
        up_grad_kernel,
        grid=(6,),
        out_shape=shape((width, inner), f32),
        in_specs=[whole, whole, part, part],
        out_specs=pl.BlockSpec((width, tile), lambda j: (0, j)),
        compiler_params=params(),
        cost_estimate=cost(10),
        name="up_gradient",
    )(buf_a, buf_b, dpre_a, dpre_b)


def run_down_grad(dout_a, dout_b, act_a, act_b):
    slots, width = dout_a.shape
    inner = act_a.shape[1]
    tile = inner // 6
    whole = pl.BlockSpec((slots, width), lambda j: (0, 0))
    part = pl.BlockSpec((slots, tile), lambda j: (0, j))
    return pl.pallas_call(
        down_grad_kernel,
        grid=(6,),
        out_shape=shape((inner, width), f32),
        in_specs=[whole, whole, part, part],
        out_specs=pl.BlockSpec((tile, width), lambda j: (j, 0)),
        compiler_params=params(),
        cost_estimate=cost(10),
        name="down_gradient",
    )(dout_a, dout_b, act_a, act_b)


def swap(block):
    return lax.ppermute(block, "section", [(0, 1), (1, 0)])


def moved(block, source):
    return lax.ppermute(block, "section", [(source, 1 - source)])


def across(block, bit, devices):
    return lax.ppermute(block, "expert", [(i, i ^ (1 << bit)) for i in range(devices)])


def bit_orders(bits):
    if bits == 4:
        return [(3, 2, 0, 1), (3, 0, 1, 2), (3, 1, 2, 0)]
    names = list(range(bits))
    return [tuple(names[(i + r * bits // pieces) % bits] for i in names) for r in range(pieces)]


def split_lanes(block):
    step = block.shape[-1] // pieces
    return [block[..., p * step : (p + 1) * step] for p in range(pieces)]


def token_of(block):
    value = block[(0,) * block.ndim]
    return (value != value).astype(jnp.int32)


def gathered(shards, device, devices, after):
    bits = devices.bit_length() - 1
    orders = bit_orders(bits)
    rows = shards[0].shape[1]
    if rows % 16:
        found = [p.reshape(p.shape[:1] + (1,) * bits + p.shape[1:]) for p in shards]
        for step in range(bits):
            for p in range(pieces):
                bit = orders[p][step]
                axis = bits - bit
                got = across(found[p], bit, devices)
                high = (device >> bit) & 1 == 1
                found[p] = jnp.where(
                    high,
                    jnp.concatenate([got, found[p]], axis),
                    jnp.concatenate([found[p], got], axis),
                )
        found = [p.reshape(1, p.shape[0], -1, p.shape[-1]) for p in found]
        passed = [[moved(p, source) for p in found] for source in range(2)]
        return [[[0]]] * pieces, False, [[*found, *other] for other in passed]
    me = device.astype(jnp.int32).reshape(1)
    found = [p[None] for p in shards]
    differ = [[0] for _ in shards]
    for step in range(bits - 1):
        gots = [across(found[p], orders[p][step], devices) for p in range(pieces)]
        outs = [shape((2 * p.shape[0],) + p.shape[1:]) for p in found]
        last = after if step == bits - 2 else ()
        found = run(join_kernel, "join", 3, [*found, *gots], outs, [], me, (), last)[1:]
        for p in range(pieces):
            differ[p] = differ[p] + [d ^ (1 << orders[p][step]) for d in differ[p]]
    far = [across(found[p], orders[p][-1], devices) for p in range(pieces)]
    layout = [
        [differ[p], [d ^ (1 << orders[p][-1]) for d in differ[p]]] for p in range(pieces)
    ]
    own = [block for couple in zip(found, far) for block in couple]
    arrays = [[*own, *[moved(block, source) for block in own]] for source in range(2)]
    return layout, True, arrays


def halved(block, bit, bits, lead, device, devices, late=0):
    axis = lead + bits - 1 - bit
    low = lax.index_in_dim(block, 0, axis, keepdims=True)
    high = lax.index_in_dim(block, 1, axis, keepdims=True)
    got = across(jnp.where((device >> bit) & 1 == 1, low, high), bit, devices)
    up = ((device + late) >> bit) & 1 == 1
    return jnp.where(up, high, low).astype(f32) + got.astype(f32)


def folded(found, step, device, devices, late=0):
    bits = devices.bit_length() - 1
    orders = [order[::-1] for order in bit_orders(bits)]
    results = []
    for p in range(pieces):
        value = halved(found[p], orders[p][step], bits, 1, device, devices, late)
        results.append(value if step == bits - 1 else value.astype(bf16))
    return results


def unfolded(total, devices):
    bits = devices.bit_length() - 1
    return [
        p.reshape(p.shape[:1] + (2,) * bits + (p.shape[1] // devices, p.shape[2]))
        for p in split_lanes(total)
    ]


def body(
    block_input,
    cotangent,
    lengths,
    routes,
    norm_gain,
    attention_in,
    attention_out,
    position_bias,
    router,
    expert_up,
    expert_down,
):
    _, rows, width = block_input.shape
    section = lax.axis_index("section")
    device = lax.axis_index("expert")
    devices = lax.axis_size("expert")
    bits = devices.bit_length() - 1
    first = section == 0
    mine = [(section == which).astype(jnp.int32).reshape(1) for which in range(2)]
    experts = router.shape[2]
    shard_rows = router.shape[1]
    buckets, heads = position_bias.shape[1:]
    most = max(2, 3 * rows // (2 * experts))
    capacity = -(-most // 8) * 8
    slots = experts * capacity

    def both(own, other):
        return (jnp.where(first, own, other), jnp.where(first, other, own))

    def own_micro(block):
        return jnp.where(first, block[0], block[1])

    def other_micro(block):
        return jnp.where(first, block[1], block[0])

    own_shards = jnp.concatenate([attention_in[0], attention_out], axis=0)
    cut = split_lanes(own_shards)
    pad = cut[0].shape[-1] - experts
    cut[0] = jnp.concatenate([cut[0], jnp.pad(router, ((0, 0), (0, 0), (0, pad)))], axis=0)
    small_parts = (
        norm_gain[0].reshape(-1),
        position_bias[0].reshape(-1),
        other_micro(routes[0])[:, 0].astype(f32),
    )
    small = jnp.concatenate(small_parts)
    small = jnp.pad(small, (0, -small.shape[0] % 128)).reshape(-1, 128)
    small_given = swap(small).reshape(-1)
    split_at, at = [], 0
    for part in small_parts:
        at += part.shape[0]
        split_at.append(at)
    gain_other, table_other, route_other, _ = jnp.split(small_given, split_at)
    gains = both(norm_gain[0], gain_other.reshape(2, width))
    tables = both(position_bias[0], table_other.reshape(buckets, heads))
    route_pair = both(own_micro(routes[0])[:, 0], route_other.astype(jnp.int32))

    positions = jnp.arange(rows, dtype=jnp.int32)
    bounds = jnp.cumsum(own_micro(lengths)[0])
    segment = jnp.sum((positions[:, None] >= bounds[None, :]).astype(jnp.int32), axis=1)
    seg_col, seg_row = segment[:, None], segment[None, :]
    offsets = jnp.arange(2 * rows, dtype=jnp.int32) - (rows - 1)
    bucket_hot = (
        bucket_of(offsets)[:, None] == jnp.arange(buckets, dtype=jnp.int32)[None, :]
    ).astype(f32)
    lines = [
        lax.dot_general(table, bucket_hot, (((0,), (1,)), ((), ())), precision=highest)
        for table in tables
    ]
    bases = [run_bias(line, rows) for line in lines]
    before = (positions[:, None] > positions[None, :]).astype(bf16)
    places = []
    for route in route_pair:
        chosen = route[:, None] == jnp.arange(experts, dtype=jnp.int32)[None, :]
        earlier = dot(before, chosen.astype(bf16))
        slot = jnp.sum(jnp.where(chosen, earlier, 0.0), axis=1).astype(jnp.int32)
        places.append(route * capacity + slot)
    route_cols = [route[:, None] for route in route_pair]
    place_cols = [place[:, None] for place in places]
    place_rows = [place[None, :] for place in places]
    layout, apart, weights = gathered(
        cut, device, devices, (place_rows[0], route_cols[0], seg_col, seg_row, gains[0])
    )
    core = jnp.stack([section, device if apart else jnp.zeros_like(device)]).astype(jnp.int32)
    up_other = swap(expert_up[0, 0])
    down_other = swap(expert_down[0, 0])
    ups, downs = (expert_up[0, 0], up_other), (expert_down[0, 0], down_other)

    def exchanged(block):
        return lax.all_to_all(block, "expert", split_axis=0, concat_axis=0, tiled=True)

    def expert_forward(which, arrived):
        return run_expert(
            expert_forward_kernel, mine[which], arrived, (), ups, downs, 2, 11, "expert_forward",
            weights[1][len(weights[1]) // 2 :] if which == 0 else (),
        )

    def expert_backward(mine, arrived, slope):
        return run_expert(
            expert_backward_kernel, mine, arrived, (slope,), ups, downs, 1, 11,
            "expert_backward",
        )

    def shared_inputs(which):
        return (
            gains[which], seg_col, seg_row, route_cols[which],
        )

    inputs = own_micro(block_input)
    cot = own_micro(cotangent)
    token, q0, k0, v0, o0, p0, mid0, h20, share0, gate0, send0 = run_forward(
        False, layout, core, [*weights[0], bases[0]], (inputs, *shared_inputs(0), place_rows[0]), slots, experts,
        heads, (),
    )
    buf0 = exchanged(send0)
    act0, slope0, result0 = expert_forward(0, buf0)
    back0 = exchanged(result0)
    _, q1, k1, v1, o1, p1, mid1, h21, share1, gate1, send1, between, combined0, grad_send1 = (
        run_forward(
            True, layout, core, [*weights[1], bases[1]],
            (mid0, gate0, place_cols[0], back0, cot, *shared_inputs(1), place_rows[1]),
            slots, experts, heads, (),
        )
    )
    buf1 = exchanged(send1)
    dout1 = exchanged(grad_send1)
    act1, slope1, result1 = expert_forward(1, buf1)
    dpre1, dbuf1 = expert_backward(mine[1], dout1, slope1)
    back1 = exchanged(
        jnp.concatenate(
            [block.reshape(experts, capacity, width)[:, :most] for block in (result1, dbuf1)], axis=1
        ).reshape(2 * experts * most, width)
    )
    place_out = place_cols[1] + route_cols[1] * (2 * most - capacity)
    _, dx11, low1, dq1, dk1, dv1, router_grad1, gain_two1, line_grad1, last = run_heads_backward(
        True, layout, core, [*weights[1], p1],
        (q1, k1, v1, mid1, h21, share1, gate1, cot, back1, place_out, gains[1],
         route_cols[1], place_out + most),
        experts, (),
    )
    token, dx1, gain_one1, dy0, grad_send0 = run_input_backward(
        True, layout, core, weights[1],
        (between, dx11, dq1, dk1, dv1, gains[1], gate0, place_rows[0]), slots, (),
    )
    token, keep1, give1 = run_weight_backward(
        core + token[0], (between, gains[1], o1, low1, dq1, dk1, dv1), ()
    )
    dout0 = exchanged(grad_send0)

    given1 = swap(give1)
    dpre0, dbuf0 = expert_backward(mine[0] + token[0], dout0, slope0)
    dback0 = exchanged(dbuf0)
    from_first = [swap(block) for block in (buf1, act1, dout1, dpre1)]
    from_second = [swap(block) for block in (buf0, act0, dout0, dpre0)]

    def up_of(bufs, dpres):
        return run_up_grad(*bufs, *dpres)

    def down_of(douts, acts):
        return run_down_grad(*douts, *acts)

    up_sets = ((buf0, from_second[0], dpre0, from_second[3]), (buf1, from_first[0], dpre1, from_first[3]))
    down_sets = ((dout0, from_second[2], act0, from_second[1]), (dout1, from_first[2], act1, from_first[1]))

    def own_layer(run_grad, sets, token):
        return lax.cond(
            section + token == 0, lambda a, b: run_grad(*a), lambda a, b: run_grad(*b), *sets
        )

    grads = [
        functools.partial(own_layer, run_down_grad, down_sets),
        functools.partial(own_layer, run_up_grad, up_sets),
    ]

    grad_down = grads[0](token_of(dbuf0))
    token, dx10, low0, dq0, dk0, dv0, router_grad0, gain_two0, line_grad0 = run_heads_backward(
        False, layout, core, [*weights[0], p0],
        (q0, k0, v0, mid0, h20, share0, gate0, dy0, dback0, combined0, gains[0],
         route_cols[0], place_cols[0]),
        experts, (grad_down,),
    )
    token, keep0, give0 = run_weight_backward(
        core, (inputs, gains[0], o0, low0, dq0, dk0, dv0), ()
    )
    _, dx0, gain_one0 = run_input_backward(
        False, layout, core + token[0], weights[0], (inputs, dx10, dq0, dk0, dv0, gains[0]), slots, ()
    )

    little = [
        jnp.concatenate(parts, axis=0)
        for parts in (
            (gain_one0, gain_two0, line_grad0, router_grad0),
            (gain_one1, gain_two1, line_grad1, router_grad1),
        )
    ]
    little = jnp.where(first, little[0], little[1]) + swap(jnp.where(first, little[1], little[0]))
    sums, little_sum, (grad_up,) = summed_blocks(
        [keep0, swap(give0), keep1, given1], little, device, devices, grads[1:], (dx0,)
    )
    shared0, shared1 = sums[:2], sums[2:]
    shared_other = swap(jnp.where(first, shared1, shared0))
    queries_keys = jnp.where(first, shared0, shared_other)
    values_out = jnp.where(first, shared_other, shared1)

    grad_table = jnp.dot(little_sum[2 : 2 + heads], bucket_hot, precision=highest).T
    router_sum = lax.dynamic_slice_in_dim(little_sum[2 + heads :], device * shard_rows, shard_rows, 1)

    out_other = swap(jnp.where(first, last, between))
    layer_out = jnp.stack(
        [jnp.where(first, between, out_other), jnp.where(first, out_other, last)]
    )
    grad_other = swap(jnp.where(first, dx1, dx0))
    input_grad = jnp.stack([jnp.where(first, dx0, grad_other), jnp.where(first, grad_other, dx1)])
    return (
        layer_out[None],
        input_grad[None],
        little_sum[:2][None],
        jnp.concatenate([queries_keys, values_out[:1]], axis=0)[None],
        values_out[1][None],
        grad_table[None],
        router_sum.T[None],
        grad_up[None, None],
        grad_down[None, None],
    )


def solution(mesh):
    in_specs = (
        P(None, "expert", None),
        P(None, "expert", None),
        P(None, "expert", None),
        P("section", None, "expert", None),
        P("section", None, None),
        P("section", None, "expert", None),
        P("section", "expert", None),
        P("section", None, None),
        P("section", "expert", None),
        P("section", "expert", None, None),
        P("section", "expert", None, None),
    )
    out_specs = (
        P("section", None, "expert", None),
        P("section", None, "expert", None),
        P("section", None, None),
        P("section", None, "expert", None),
        P("section", "expert", None),
        P("section", None, None),
        P("section", "expert", None),
        P("section", "expert", None, None),
        P("section", "expert", None, None),
    )
    return jax.shard_map(body, mesh=mesh, in_specs=in_specs, out_specs=out_specs, check_vma=False)
```
